768 devices in a mesh: dp: 24 (over z, core), mp: 8 (over y), rep: 4 (over x).
Axes of the slice: x: 4, y: 8, z: 12, core: 2. Of those that a mesh axis runs over, the one named last changes fastest.
Arguments:
- tokens: bfloat16 [24576, 256], P(('dp', 'rep')), may hold values from -6 to 6
- cotangent: bfloat16 [24576, 53248], P(('dp', 'rep'), 'mp'), may hold values from -0.0390625 to 0.0390625
- token_counts: int32 [24, 4], P('dp', 'rep'), may hold values from 128 to 256, as said below
- old_bounds: int32 [8, 24, 2], P('mp', 'dp'), may hold values from 0 to 1916928, as said below
- old_first: float32 [8, 3833856], P('mp', 'dp'), may hold values from -3 to 3
- old_second: float32 [8, 3833856], P('mp', 'dp'), may hold values from 0.05 to 2
- old_master: float32 [8, 3833856], P('mp', 'dp'), may hold values from -6 to 6
Outputs:
- new_master: float32 [8, 1916928], P('mp', 'dp')
- new_first: float32 [8, 1916928], P('mp', 'dp')
- new_second: float32 [8, 1916928], P('mp', 'dp')
The draws below stay inside these ranges and needn't reach their ends.
Inputs may be any that keep to these rules, and one draw needn't show every extreme that they name: `old_bounds`: for each slab s, row j holds the boundaries b_j and b_(j+1) of that slab's list with b_0 = 0 and b_(24) = 1916928; every b_j lies within 33280 of j * 79872; some b_j lies exactly 33280 away from it. `token_counts`: some data rank has all 256 tokens live.
All inputs are finite; a program needn't handle non-finite values.
Results may differ from the reference program's by a relative error of at most 0.0003.
Values sent between devices are 32-bit elements; how exact they have to be, the bound alone decides.
No kernel may reach another device: no remote copies, remote signals or barrier semaphores. Data moves between devices by JAX's collectives and lax.ppermute only.
A program may use at most 64 MiB of HBM per device.

```python
import math
import jax
import jax.numpy as jnp
from jax import lax

COLS = 6656
BROWS = 256
TOK_DEV = 256
ADAM_STEP = 1000
SHARDS = 24
REPS = 4
SLABS = 8
TOKENS = 24576
SLAB = 1703936
P_SIZE = 79872
HALF = 33280
CAP = 159744


def draw_old_bounds(key, part):
    key = jax.random.fold_in(key, 11)
    offsets = jax.random.randint(key, (SLABS, SHARDS + 1), -HALF, HALF + 1)
    places = jnp.arange(SHARDS + 1, dtype=jnp.int32)[None, :]
    slab_ids = jnp.arange(SLABS, dtype=jnp.int32)[:, None]
    signs = jnp.where(slab_ids % 2 == 0, 1, -1)
    edge = (places == 1) | (places == SHARDS - 1)
    offsets = jnp.where(edge, signs * HALF, offsets)
    offsets = jnp.where((places == 0) | (places == SHARDS), 0, offsets)
    bounds = places * P_SIZE + offsets
    return jnp.stack([bounds[:, :-1], bounds[:, 1:]], axis=2).astype(jnp.int32)


def draw_token_counts(key, part):
    key = jax.random.fold_in(key, 23)
    key_a, key_b = jax.random.split(key)
    values = jax.random.randint(key_a, (SHARDS * REPS,), TOK_DEV // 2, TOK_DEV + 1)
    chosen = jax.random.randint(key_b, (), 0, SHARDS * REPS)
    places = jnp.arange(SHARDS * REPS, dtype=jnp.int32)
    values = jnp.where(places == chosen, TOK_DEV, values)
    return values.reshape(SHARDS, REPS).astype(jnp.int32)


def shard_levels(rng, shape, pieces, least, high):
    def one(dim, shards_of):
        steps = jax.random.uniform(jax.random.fold_in(jax.random.fold_in(rng, 6), dim), (shards_of,), jnp.float32, least / len(pieces), high / len(pieces))
        return jnp.repeat(jnp.exp(steps), shape[dim] // shards_of).reshape((-1,) + (1,) * (len(shape) - dim - 1))

    loudness = one(*pieces[0])
    for cut in pieces[1:]:
        loudness = loudness * one(*cut)
    return loudness


def normal_values(key, shape, scale, bound, shards=(), held_as=jnp.bfloat16):
    level = shard_levels(key, shape, shards, -0.22, 0.18) if shards else 1.0
    values = jax.random.normal(key, shape, jnp.float32) * scale * level
    return jnp.minimum(jnp.maximum(values, -bound), bound).astype(held_as)


def setup_inputs(seed: int = 0) -> dict:
    keys = jax.random.split(jax.random.key(seed), 8)
    tokens = normal_values(keys[0], (TOKENS, BROWS), 1.0, 6.0, ((0, 96),))
    cotangent = normal_values(keys[1], (TOKENS, SLABS * COLS), TOKENS ** -0.5, 0.0390625, ((0, 96), (1, 8)))
    token_counts = draw_token_counts(jax.random.fold_in(keys[7], 71), 0)
    old_bounds = draw_old_bounds(jax.random.fold_in(keys[7], 71), 0)
    old_first = normal_values(keys[4], (SLABS, SHARDS * CAP), 0.3, 3.0, ((0, 8), (1, 24)), jnp.float32)
    old_second = jnp.clip(jnp.exp(math.log(2.0) - 3.6888794 * jax.random.uniform(keys[5], (SLABS, SHARDS * CAP), jnp.float32) ** shard_levels(keys[5], (SLABS, SHARDS * CAP), ((0, 8), (1, 24)), -0.2, 0.2)), 0.05, 2.0)
    old_master = normal_values(keys[6], (SLABS, SHARDS * CAP), 1.0, 6.0, ((0, 8), (1, 24)), jnp.float32)
    return {"tokens": tokens, "cotangent": cotangent, "token_counts": token_counts, "old_bounds": old_bounds, "old_first": old_first, "old_second": old_second, "old_master": old_master}


BETA_ONE = 0.9
BETA_TWO = 0.95
LEARN_RATE = 0.001
DECAY_RATE = 0.1
EPSILON = 1e-08

def adam_step(first, second, master, gradient):
    first_new = BETA_ONE * first + (1.0 - BETA_ONE) * gradient
    second_new = BETA_TWO * second + (1.0 - BETA_TWO) * gradient * gradient
    corr_one = 1.0 - BETA_ONE ** ADAM_STEP
    corr_two = 1.0 - BETA_TWO ** ADAM_STEP
    update = first_new / corr_one / (jnp.sqrt(second_new / corr_two) + EPSILON) + DECAY_RATE * master
    return (master - LEARN_RATE * update, first_new, second_new)

def regroup(bounds, first_row, second_row, master_row):
    positions = jnp.arange(SHARDS * P_SIZE, dtype=jnp.int32)
    lower_ends = bounds[:, 0].astype(jnp.int32)
    owners = (jnp.searchsorted(lower_ends, positions, side='right') - 1).astype(jnp.int32)
    gather_index = (owners * CAP + positions - lower_ends[owners]).astype(jnp.int32)
    return (first_row[gather_index], second_row[gather_index], master_row[gather_index])

def reference(tokens, cotangent, token_counts, old_bounds, old_first, old_second, old_master):
    row_ids = jnp.arange(TOKENS, dtype=jnp.int32)
    limits = jnp.repeat(token_counts.reshape(-1), TOK_DEV)
    live_rows = row_ids % TOK_DEV < limits
    masked = jnp.where(live_rows[:, None], tokens, jnp.zeros_like(tokens))
    gradient = lax.dot_general(masked, cotangent, (((0,), (0,)), ((), ())), preferred_element_type=jnp.float32)
    gradient = gradient.reshape(BROWS, SLABS, COLS).transpose(1, 0, 2).reshape(SLABS, SLAB)
    flat_grad = jnp.pad(gradient, ((0, 0), (0, SHARDS * P_SIZE - SLAB)))
    first, second, master = jax.vmap(regroup)(old_bounds, old_first, old_second, old_master)
    new_master, new_first, new_second = adam_step(first, second, master, flat_grad)
    return (new_master, new_first, new_second)
```

```python
import functools

import jax
import jax.numpy as jnp
from jax import lax
from jax.experimental import pallas as pl
from jax.experimental.pallas import tpu as pltpu
from jax.sharding import PartitionSpec as P

ADAM_STEP = 1000
BETA_ONE = 0.9
BETA_TWO = 0.95
LEARN_RATE = 0.001
DECAY_RATE = 0.1
EPSILON = 1e-08

SHARDS = 24
COLS = 6656
BROWS = 256
LANES = 128
P_SIZE = 79872
HALF = 33280
CAP = 159744
ROWS = P_SIZE // LANES
HROWS = HALF // LANES
CROWS = CAP // LANES
FRONT = 264
SROWS = 39
SCOLS = 2048
STEP_COLS = 512
GROWS = P_SIZE // COLS


def grad_kernel(count_ref, tok_ref, c0_ref, c1_ref, c2_ref, c3_ref, out_ref, lhs_ref):
    step = pl.program_id(0)
    total = SHARDS * SROWS
    tok_row = lax.broadcasted_iota(jnp.int32, (BROWS, BROWS), 0)
    tok = jnp.where(tok_row < count_ref[0], tok_ref[...], jnp.zeros_like(tok_ref))
    row = lax.broadcasted_iota(jnp.int32, (total, BROWS), 0)
    col = lax.broadcasted_iota(jnp.int32, (total, BROWS), 1)
    shard = lax.shift_right_logical(row * 1681, 16)
    inner = row - shard * SROWS
    lead = col - shard * GROWS

    def picked(match):
        one = jnp.where(match, jnp.float32(1), jnp.float32(0)).astype(jnp.bfloat16)
        out = lax.dot_general(one, tok, (((1,), (1,)), ((), ())), preferred_element_type=jnp.float32)
        return out.astype(jnp.bfloat16)

    @pl.when(step == 0)
    def _():
        for q in range(3):
            fits = (inner >= GROWS * q) & (inner < GROWS * (q + 1))
            lhs_ref[q] = picked(fits & (lead == inner - GROWS * q))

    last = picked((inner >= 36) & (lead == 4 * (inner - 36) + step))

    def dot(a, b):
        return jnp.dot(a, b[...], preferred_element_type=jnp.float32)

    acc = dot(lhs_ref[0], c0_ref) + dot(lhs_ref[1], c1_ref)
    out_ref[...] = acc + dot(lhs_ref[2], c2_ref) + dot(last, c3_ref)


def local_gradient(tokens, cotangent, count):
    block = (BROWS, STEP_COLS)
    return pl.pallas_call(
        grad_kernel,
        grid=(4,),
        in_specs=[
            pl.BlockSpec(memory_space=pltpu.SMEM),
            pl.BlockSpec((BROWS, BROWS), lambda k: (0, 0)),
            pl.BlockSpec(block, lambda k: (0, k)),
            pl.BlockSpec(block, lambda k: (0, 4 + k)),
            pl.BlockSpec(block, lambda k: (0, 8 + k)),
            pl.BlockSpec(block, lambda k: (0, 12)),
        ],
        out_specs=pl.BlockSpec((SHARDS * SROWS, STEP_COLS), lambda k: (0, k)),
        out_shape=jax.ShapeDtypeStruct((SHARDS * SROWS, SCOLS), jnp.float32),
        scratch_shapes=[pltpu.VMEM((3, SHARDS * SROWS, BROWS), jnp.bfloat16)],
        compiler_params=pltpu.CompilerParams(vmem_limit_bytes=56 * 1024 * 1024),
        cost_estimate=pl.CostEstimate(flops=4 * 10**9, bytes_accessed=11 * 10**6, transcendentals=0),
    )(count, tokens, cotangent, cotangent, cotangent, cotangent)


def shifted(ref, start, rows):
    start = start + FRONT * LANES
    top = lax.shift_right_logical(start, 7)
    lane_start = start - top * LANES
    first = pltpu.roll(ref[pl.ds(top, rows), :], LANES - lane_start, 1)
    second = pltpu.roll(ref[pl.ds(top + 1, rows), :], LANES - lane_start, 1)
    lane = lax.broadcasted_iota(jnp.int32, (rows, LANES), 1)
    return jnp.where(lane < LANES - lane_start, first, second)


def load_old(refs, buf, sem):
    copies = [pltpu.make_async_copy(r, buf.at[i, pl.ds(FRONT, CROWS)], sem.at[i]) for i, r in enumerate(refs)]
    for c in copies:
        c.start()
    for i in range(3):
        buf[i, :FRONT, :] = jnp.zeros((FRONT, LANES), jnp.float32)
        buf[i, FRONT + CROWS :, :] = jnp.zeros((8, LANES), jnp.float32)
    for c in copies:
        c.wait()


def halo_kernel(place_ref, a_ref, b_ref, c_ref, right_ref, left_ref, buf, sem):
    load_old((a_ref, b_ref, c_ref), buf, sem)
    ahead = lax.axis_index("dp") * P_SIZE - place_ref[0]
    for i in range(3):
        right_ref[i] = shifted(buf.at[i], ahead + P_SIZE, HROWS)
        left_ref[i] = shifted(buf.at[i], jnp.maximum(ahead, 0) - HALF, HROWS)


def state_kernel(place_ref, a_ref, b_ref, c_ref, left_ref, right_ref, out_ref, buf, sem):
    load_old((a_ref, b_ref, c_ref), buf, sem)
    base = lax.axis_index("dp") * P_SIZE
    lower, upper = place_ref[0], place_ref[1]
    row = lax.broadcasted_iota(jnp.int32, (ROWS, LANES), 0)
    lane = lax.broadcasted_iota(jnp.int32, (ROWS, LANES), 1)
    pos = base + row * LANES + lane
    tail = ROWS - HROWS
    for i in range(3):
        own = shifted(buf.at[i], base - lower, ROWS)
        out_ref[i] = own
        out_ref[i, :HROWS, :] = jnp.where(pos[:HROWS] < lower, left_ref[i], own[:HROWS])
        out_ref[i, tail:, :] = jnp.where(pos[tail:] >= upper, right_ref[i], own[tail:])


OLD_SCRATCH = (
    pltpu.VMEM((3, FRONT + CROWS + 8, LANES), jnp.float32),
    pltpu.SemaphoreType.DMA((3,)),
)
SMEM_SPEC = pl.BlockSpec(memory_space=pltpu.SMEM)
ANY_SPEC = pl.BlockSpec(memory_space=pl.ANY)
VMEM_SPEC = pl.BlockSpec(memory_space=pltpu.VMEM)


def halos(place, old):
    shape = jax.ShapeDtypeStruct((3, HROWS, LANES), jnp.float32)
    return pl.pallas_call(
        halo_kernel,
        in_specs=[SMEM_SPEC, ANY_SPEC, ANY_SPEC, ANY_SPEC],
        out_specs=(VMEM_SPEC, VMEM_SPEC),
        out_shape=(shape, shape),
        scratch_shapes=list(OLD_SCRATCH),
        cost_estimate=pl.CostEstimate(flops=10**6, bytes_accessed=3 * 10**6, transcendentals=0),
    )(place, *old)


def new_state(place, old, left, right):
    return pl.pallas_call(
        state_kernel,
        in_specs=[SMEM_SPEC, ANY_SPEC, ANY_SPEC, ANY_SPEC, VMEM_SPEC, VMEM_SPEC],
        out_specs=VMEM_SPEC,
        out_shape=jax.ShapeDtypeStruct((3, ROWS, LANES), jnp.float32),
        scratch_shapes=list(OLD_SCRATCH),
        cost_estimate=pl.CostEstimate(flops=10**6, bytes_accessed=4 * 10**6, transcendentals=0),
    )(place, *old, left, right)


def adam_kernel(s0_ref, s1_ref, t0_ref, t1_ref, state_ref, master_ref, first_ref, second_ref, grad):
    tiles = COLS // LANES
    for half, (s, t) in enumerate(((s0_ref, t0_ref), (s1_ref, t1_ref))):
        for j in range(8):
            at = 8 * half + j
            piece = s[:, LANES * j : LANES * (j + 1)] + t[:, LANES * j : LANES * (j + 1)]
            for q in range(3):
                grad[pl.ds(16 * q + at, GROWS, stride=tiles), :] = piece[GROWS * q : GROWS * (q + 1)]
            k, c = at // 4, at % 4
            grad[pl.ds(tiles * k + 48 + c, 3, stride=4 * tiles), :] = piece[36:39]
    corr_one = 1.0 - BETA_ONE**ADAM_STEP
    corr_two = 1.0 - BETA_TWO**ADAM_STEP
    g = grad[...]
    first_new = BETA_ONE * state_ref[0] + (1.0 - BETA_ONE) * g
    second_new = BETA_TWO * state_ref[1] + (1.0 - BETA_TWO) * g * g
    master = state_ref[2]
    update = first_new / corr_one / (jnp.sqrt(second_new / corr_two) + EPSILON) + DECAY_RATE * master
    master_ref[...] = master - LEARN_RATE * update
    first_ref[...] = first_new
    second_ref[...] = second_new


def adam_step(parts, state):
    shape = jax.ShapeDtypeStruct((ROWS, LANES), jnp.float32)
    return pl.pallas_call(
        adam_kernel,
        in_specs=[VMEM_SPEC] * 5,
        out_specs=(VMEM_SPEC,) * 3,
        out_shape=(shape,) * 3,
        scratch_shapes=[pltpu.VMEM((ROWS, LANES), jnp.float32)],
        cost_estimate=pl.CostEstimate(flops=2 * 10**6, bytes_accessed=3 * 10**6, transcendentals=10**5),
    )(*parts, state)


def local(tokens, cotangent, token_counts, old_bounds, old_first, old_second, old_master):
    place = old_bounds.reshape(2)
    old = [a.reshape(CROWS, LANES) for a in (old_first, old_second, old_master)]
    to_right, to_left = halos(place, old)
    left_in = lax.ppermute(to_right, "dp", [(i, i + 1) for i in range(SHARDS - 1)])
    right_in = lax.ppermute(to_left, "dp", [(i + 1, i) for i in range(SHARDS - 1)])

    partial = local_gradient(tokens, cotangent, token_counts.reshape(1))
    shard = lax.psum_scatter(partial, "dp", scatter_dimension=0, tiled=True)
    shard = lax.optimization_barrier(shard)

    low = [(0, 1), (1, 0), (2, 3), (3, 2)]
    high = [(1, 2), (2, 1), (3, 0), (0, 3)]
    s0, s1 = shard[:, : SCOLS // 2], shard[:, SCOLS // 2 :]
    s0 = s0 + lax.ppermute(s0, "rep", low)
    s1 = s1 + lax.ppermute(s1, "rep", high)
    t0 = lax.ppermute(s0, "rep", high)
    t1 = lax.ppermute(s1, "rep", low)

    state = new_state(place, old, left_in, right_in)
    outs = adam_step((s0, s1, t0, t1), state)
    return tuple(a.reshape(1, P_SIZE) for a in outs)


def solution(mesh):
    placed = (
        P(("dp", "rep"), None),
        P(("dp", "rep"), "mp"),
        P("dp", "rep"),
        P("mp", "dp", None),
        P("mp", "dp"),
        P("mp", "dp"),
        P("mp", "dp"),
    )
    return jax.shard_map(
        local,
        mesh=mesh,
        in_specs=placed,
        out_specs=(P("mp", "dp"), P("mp", "dp"), P("mp", "dp")),
        check_vma=False,
    )
```

```python
import functools

import jax
import jax.numpy as jnp
import numpy as np
from jax import lax
from jax.experimental import pallas as pl
from jax.experimental.pallas import tpu as pltpu
from jax.sharding import PartitionSpec as P

ADAM_STEP = 1000
BETA_ONE = 0.9
BETA_TWO = 0.95
LEARN_RATE = 0.001
DECAY_RATE = 0.1
EPSILON = 1e-08

SHARDS = 24
COLS = 6656
BROWS = 256
LANES = 128
P_SIZE = 79872
HALF = 33280
CAP = 159744
ROWS = P_SIZE // LANES
HROWS = HALF // LANES
CROWS = CAP // LANES
FRONT = 264
SROWS = 39
SCOLS = 2048
STEP_COLS = 512
GROWS = P_SIZE // COLS


def row_class(row):
    return min(row % SROWS // GROWS, 3)


TOTAL = SHARDS * SROWS
TILES_OF = [sorted({row // 8 for row in range(TOTAL) if row_class(row) == c}) for c in range(4)]
PART_ROWS = [(8 * len(tiles) + 15) // 16 * 16 for tiles in TILES_OF]
PART_AT = [sum(PART_ROWS[:c]) for c in range(4)]
PICK_ROWS = sum(PART_ROWS) + 3 * PART_ROWS[3]


def row_picks():
    picks = np.zeros((PICK_ROWS, BROWS), np.float32)
    for c in range(4):
        for i, tile in enumerate(TILES_OF[c]):
            for row in range(8 * tile, 8 * tile + 8):
                if row_class(row) != c:
                    continue
                shard, inner = row // SROWS, row % SROWS
                at = PART_AT[c] + 8 * i + row % 8
                for step in range(4 if c == 3 else 1):
                    token_col = GROWS * shard + (4 * (inner - 36) + step if c == 3 else inner - GROWS * c)
                    if token_col < BROWS:
                        picks[at + step * PART_ROWS[3], token_col] = 1
    return picks.astype(jnp.bfloat16)


def grad_kernel(count_ref, tok_ref, pick_ref, c0_ref, c1_ref, c2_ref, c3_ref, out_ref, lhs_ref, part_ref):
    step = pl.program_id(0)

    @pl.when(step == 0)
    def _():
        tok_row = lax.broadcasted_iota(jnp.int32, (BROWS, BROWS), 0)
        tok = jnp.where(tok_row < count_ref[0], tok_ref[...], jnp.zeros_like(tok_ref))
        lhs_ref[...] = lax.dot_general(
            pick_ref[...], tok, (((1,), (1,)), ((), ())), preferred_element_type=jnp.float32
        ).astype(jnp.bfloat16)

    for c, cot in enumerate((c0_ref, c1_ref, c2_ref, c3_ref)):
        start = PART_AT[c] if c < 3 else pl.multiple_of(PART_AT[3] + step * PART_ROWS[3], 16)
        lhs = lhs_ref[pl.ds(start, PART_ROWS[c]), :]
        part_ref[pl.ds(PART_AT[c], PART_ROWS[c]), :] = jnp.dot(
            lhs, cot[...], preferred_element_type=jnp.float32
        )
    for tile in range(TOTAL // 8):
        found = [PART_AT[c] + 8 * TILES_OF[c].index(tile) for c in range(4) if tile in TILES_OF[c]]
        out_ref[8 * tile : 8 * tile + 8, :] = sum(part_ref[at : at + 8, :] for at in found)


def local_gradient(tokens, cotangent, count):
    block = (BROWS, STEP_COLS)
    return pl.pallas_call(
        grad_kernel,
        grid=(4,),
        in_specs=[
            pl.BlockSpec(memory_space=pltpu.SMEM),
            pl.BlockSpec((BROWS, BROWS), lambda k: (0, 0)),
            pl.BlockSpec((PICK_ROWS, BROWS), lambda k: (0, 0)),
            pl.BlockSpec(block, lambda k: (0, k)),
            pl.BlockSpec(block, lambda k: (0, 4 + k)),
            pl.BlockSpec(block, lambda k: (0, 8 + k)),
            pl.BlockSpec(block, lambda k: (0, 12)),
        ],
        out_specs=pl.BlockSpec((TOTAL, STEP_COLS), lambda k: (0, k)),
        out_shape=jax.ShapeDtypeStruct((TOTAL, SCOLS), jnp.float32),
        scratch_shapes=[
            pltpu.VMEM((PICK_ROWS, BROWS), jnp.bfloat16),
            pltpu.VMEM((sum(PART_ROWS), STEP_COLS), jnp.float32),
        ],
        compiler_params=pltpu.CompilerParams(vmem_limit_bytes=56 * 1024 * 1024),
        cost_estimate=pl.CostEstimate(flops=2 * 10**9, bytes_accessed=12 * 10**6, transcendentals=0),
    )(count, tokens, jnp.asarray(row_picks()), cotangent, cotangent, cotangent, cotangent)


def shifted(ref, start, rows):
    start = start + FRONT * LANES
    top = lax.shift_right_logical(start, 7)
    lane_start = start - top * LANES
    first = pltpu.roll(ref[pl.ds(top, rows), :], LANES - lane_start, 1)
    second = pltpu.roll(ref[pl.ds(top + 1, rows), :], LANES - lane_start, 1)
    lane = lax.broadcasted_iota(jnp.int32, (rows, LANES), 1)
    return jnp.where(lane < LANES - lane_start, first, second)


def load_old(refs, buf, sem):
    copies = [pltpu.make_async_copy(r, buf.at[i, pl.ds(FRONT, CROWS)], sem.at[i]) for i, r in enumerate(refs)]
    for c in copies:
        c.start()
    for i in range(3):
        buf[i, :FRONT, :] = jnp.zeros((FRONT, LANES), jnp.float32)
        buf[i, FRONT + CROWS :, :] = jnp.zeros((8, LANES), jnp.float32)
    for c in copies:
        c.wait()


def window_kernel(bounds_ref, a_ref, b_ref, c_ref, inner_ref, outer_ref, own_ref, buf, sem):
    load_old((a_ref, b_ref, c_ref), buf, sem)
    dp = lax.axis_index("dp")
    core = lax.bitwise_and(dp, 1)
    ahead = dp * P_SIZE - bounds_ref[0]
    to_right, to_left = ahead + P_SIZE, jnp.maximum(ahead, 0) - HALF
    for i in range(3):
        inner_ref[i] = shifted(buf.at[i], jnp.where(core == 0, to_right, to_left), HROWS)
        outer_ref[i] = shifted(buf.at[i], jnp.where(core == 0, to_left, to_right), HROWS)
        own_ref[i] = shifted(buf.at[i], ahead, ROWS)


OLD_SCRATCH = (
    pltpu.VMEM((3, FRONT + CROWS + 8, LANES), jnp.float32),
    pltpu.SemaphoreType.DMA((3,)),
)
SMEM_SPEC = pl.BlockSpec(memory_space=pltpu.SMEM)
ANY_SPEC = pl.BlockSpec(memory_space=pl.ANY)
VMEM_SPEC = pl.BlockSpec(memory_space=pltpu.VMEM)


def windows(bounds, old):
    halo = jax.ShapeDtypeStruct((3, HROWS, LANES), jnp.float32)
    own = jax.ShapeDtypeStruct((3, ROWS, LANES), jnp.float32)
    return pl.pallas_call(
        window_kernel,
        in_specs=[SMEM_SPEC, ANY_SPEC, ANY_SPEC, ANY_SPEC],
        out_specs=(VMEM_SPEC,) * 3,
        out_shape=(halo, halo, own),
        scratch_shapes=list(OLD_SCRATCH),
        cost_estimate=pl.CostEstimate(flops=10**6, bytes_accessed=16 * 10**6, transcendentals=0),
    )(bounds, *old)


def adam_kernel(
    bounds_ref, s_ref, t_ref, own_ref, inner_ref, outer_ref, master_ref, first_ref, second_ref, grad, state
):
    row = lax.broadcasted_iota(jnp.int32, (ROWS, LANES), 0)
    lane = lax.broadcasted_iota(jnp.int32, (ROWS, LANES), 1)
    pos = lax.axis_index("dp") * P_SIZE + row * LANES + lane
    tail = ROWS - HROWS
    first_core = lax.bitwise_and(lax.axis_index("dp"), 1) == 0
    below, above = pos[:HROWS] < bounds_ref[0], pos[tail:] >= bounds_ref[1]
    for i in range(3):
        left = jnp.where(first_core, outer_ref[i], inner_ref[i])
        right = jnp.where(first_core, inner_ref[i], outer_ref[i])
        state[i, :HROWS, :] = jnp.where(below, left, own_ref[i, :HROWS, :])
        state[i, HROWS:tail, :] = own_ref[i, HROWS:tail, :]
        state[i, tail:, :] = jnp.where(above, right, own_ref[i, tail:, :])
    tiles = COLS // LANES
    for at in range(16):
        cols = slice(LANES * at, LANES * (at + 1))
        piece = s_ref[:, cols] + t_ref[:, cols]
        for q in range(3):
            grad[pl.ds(16 * q + at, GROWS, stride=tiles), :] = piece[GROWS * q : GROWS * (q + 1)]
        k, c = at // 4, at % 4
        grad[pl.ds(tiles * k + 48 + c, 3, stride=4 * tiles), :] = piece[36:39]
    corr_one = 1.0 - BETA_ONE**ADAM_STEP
    corr_two = 1.0 - BETA_TWO**ADAM_STEP
    g = grad[...]
    first_new = BETA_ONE * state[0] + (1.0 - BETA_ONE) * g
    second_new = BETA_TWO * state[1] + (1.0 - BETA_TWO) * g * g
    master = state[2]
    update = first_new / corr_one / (jnp.sqrt(second_new / corr_two) + EPSILON) + DECAY_RATE * master
    master_ref[...] = master - LEARN_RATE * update
    first_ref[...] = first_new
    second_ref[...] = second_new


def adam_step(bounds, parts, own, left, right):
    shape = jax.ShapeDtypeStruct((ROWS, LANES), jnp.float32)
    return pl.pallas_call(
        adam_kernel,
        in_specs=[SMEM_SPEC] + [VMEM_SPEC] * 5,
        out_specs=(VMEM_SPEC,) * 3,
        out_shape=(shape,) * 3,
        scratch_shapes=[
            pltpu.VMEM((ROWS, LANES), jnp.float32),
            pltpu.VMEM((3, ROWS, LANES), jnp.float32),
        ],
        cost_estimate=pl.CostEstimate(flops=2 * 10**6, bytes_accessed=3 * 10**6, transcendentals=10**5),
    )(bounds, *parts, own, left, right)


def rep_pairs(move0, move1):
    return [(4 * d + r, 4 * d + (move1 if d % 2 else move0)(r)) for d in range(SHARDS) for r in range(4)]


def local(tokens, cotangent, token_counts, old_bounds, old_first, old_second, old_master):
    bounds = old_bounds.reshape(2)
    old = [a.reshape(CROWS, LANES) for a in (old_first, old_second, old_master)]
    inner, outer, own = windows(bounds, old)
    inner = lax.ppermute(inner, "dp", [(i, i ^ 1) for i in range(SHARDS)])
    outer = lax.ppermute(outer, "dp", [(i, i + 1 if i % 2 else i - 1) for i in range(1, SHARDS - 1)])
    partial = local_gradient(tokens, cotangent, token_counts.reshape(1))
    shard = lax.psum_scatter(partial, "dp", scatter_dimension=0, tiled=True)
    shard = lax.optimization_barrier(shard)
    one, three = (lambda r: r ^ 1), (lambda r: r ^ 3)
    half = shard + lax.ppermute(shard, ("dp", "rep"), rep_pairs(one, three))
    rest = lax.ppermute(half, ("dp", "rep"), rep_pairs(three, one))
    outs = adam_step(bounds, (half, rest), own, inner, outer)
    return tuple(a.reshape(1, P_SIZE) for a in outs)


def solution(mesh):
    placed = (
        P(("dp", "rep"), None),
        P(("dp", "rep"), "mp"),
        P("dp", "rep"),
        P("mp", "dp", None),
        P("mp", "dp"),
        P("mp", "dp"),
        P("mp", "dp"),
    )
    return jax.shard_map(
        local,
        mesh=mesh,
        in_specs=placed,
        out_specs=(P("mp", "dp"), P("mp", "dp"), P("mp", "dp")),
        check_vma=False,
    )
```

```python
import functools

import jax
import jax.numpy as jnp
import numpy as np
from jax import lax
from jax.experimental import pallas as pl
from jax.experimental.pallas import tpu as pltpu
from jax.sharding import PartitionSpec as P

ADAM_STEP = 1000
BETA_ONE = 0.9
BETA_TWO = 0.95
LEARN_RATE = 0.001
DECAY_RATE = 0.1
EPSILON = 1e-08

SHARDS = 24
COLS = 6656
BROWS = 256
LANES = 128
P_SIZE = 79872
HALF = 33280
CAP = 159744
ROWS = P_SIZE // LANES
HROWS = HALF // LANES
CROWS = CAP // LANES
FRONT = 264
SROWS = 39
SCOLS = 2048
STEP_COLS = 512
GROWS = P_SIZE // COLS


def row_class(row):
    return min(row % SROWS // GROWS, 3)


TOTAL = SHARDS * SROWS
TILES_OF = [sorted({row // 8 for row in range(TOTAL) if row_class(row) == c}) for c in range(4)]
PART_ROWS = [(8 * len(tiles) + 15) // 16 * 16 for tiles in TILES_OF]
PART_AT = [sum(PART_ROWS[:c]) for c in range(4)]
PICK_ROWS = sum(PART_ROWS) + 3 * PART_ROWS[3]


def row_picks():
    picks = np.zeros((PICK_ROWS, BROWS), np.float32)
    for c in range(4):
        for i, tile in enumerate(TILES_OF[c]):
            for row in range(8 * tile, 8 * tile + 8):
                if row_class(row) != c:
                    continue
                shard, inner = row // SROWS, row % SROWS
                at = PART_AT[c] + 8 * i + row % 8
                for step in range(4 if c == 3 else 1):
                    token_col = GROWS * shard + (4 * (inner - 36) + step if c == 3 else inner - GROWS * c)
                    if token_col < BROWS:
                        picks[at + step * PART_ROWS[3], token_col] = 1
    return picks.astype(jnp.bfloat16)


def grad_kernel(count_ref, tok_ref, pick_ref, c0_ref, c1_ref, c2_ref, c3_ref, out_ref, lhs_ref, part_ref):
    step = pl.program_id(0)

    @pl.when(step == 0)
    def _():
        tok_row = lax.broadcasted_iota(jnp.int32, (BROWS, BROWS), 0)
        tok = jnp.where(tok_row < count_ref[0], tok_ref[...], jnp.zeros_like(tok_ref))
        lhs_ref[...] = lax.dot_general(
            pick_ref[...], tok, (((1,), (1,)), ((), ())), preferred_element_type=jnp.float32
        ).astype(jnp.bfloat16)

    for c, cot in enumerate((c0_ref, c1_ref, c2_ref, c3_ref)):
        start = PART_AT[c] if c < 3 else pl.multiple_of(PART_AT[3] + step * PART_ROWS[3], 16)
        lhs = lhs_ref[pl.ds(start, PART_ROWS[c]), :]
        part_ref[pl.ds(PART_AT[c], PART_ROWS[c]), :] = jnp.dot(
            lhs, cot[...], preferred_element_type=jnp.float32
        )
    for tile in range(TOTAL // 8):
        found = [PART_AT[c] + 8 * TILES_OF[c].index(tile) for c in range(4) if tile in TILES_OF[c]]
        out_ref[8 * tile : 8 * tile + 8, :] = sum(part_ref[at : at + 8, :] for at in found)


def local_gradient(tokens, cotangent, count):
    block = (BROWS, STEP_COLS)
    return pl.pallas_call(
        grad_kernel,
        grid=(4,),
        in_specs=[
            pl.BlockSpec(memory_space=pltpu.SMEM),
            pl.BlockSpec((BROWS, BROWS), lambda k: (0, 0)),
            pl.BlockSpec((PICK_ROWS, BROWS), lambda k: (0, 0)),
            pl.BlockSpec(block, lambda k: (0, k)),
            pl.BlockSpec(block, lambda k: (0, 4 + k)),
            pl.BlockSpec(block, lambda k: (0, 8 + k)),
            pl.BlockSpec(block, lambda k: (0, 12)),
        ],
        out_specs=pl.BlockSpec((TOTAL, STEP_COLS), lambda k: (0, k)),
        out_shape=jax.ShapeDtypeStruct((TOTAL, SCOLS), jnp.float32),
        scratch_shapes=[
            pltpu.VMEM((PICK_ROWS, BROWS), jnp.bfloat16),
            pltpu.VMEM((sum(PART_ROWS), STEP_COLS), jnp.float32),
        ],
        compiler_params=pltpu.CompilerParams(vmem_limit_bytes=56 * 1024 * 1024),
        cost_estimate=pl.CostEstimate(flops=2 * 10**9, bytes_accessed=12 * 10**6, transcendentals=0),
    )(count, tokens, jnp.asarray(row_picks()), cotangent, cotangent, cotangent, cotangent)


def shifted(ref, start, rows):
    top = lax.shift_right_logical(start, 7)
    lane_start = start - top * LANES
    first = pltpu.roll(ref[pl.ds(top, rows), :], LANES - lane_start, 1)
    second = pltpu.roll(ref[pl.ds(top + 1, rows), :], LANES - lane_start, 1)
    lane = lax.broadcasted_iota(jnp.int32, (rows, LANES), 1)
    return jnp.where(lane < LANES - lane_start, first, second)


HALO_LOAD = HROWS + 12
OWN_LOAD = ROWS + 8


def tile_row(start):
    return pl.multiple_of(lax.shift_left(lax.shift_right_arithmetic(start, 10), 3), 8)


def halo_kernel(bounds_ref, a_ref, b_ref, c_ref, inner_ref, outer_ref, ahead_buf, behind_buf, sem):
    dp = lax.axis_index("dp")
    core = lax.bitwise_and(dp, 1)
    ahead = dp * P_SIZE - bounds_ref[0]
    to_right, to_left = ahead + P_SIZE, jnp.maximum(ahead, 0) - HALF
    right_row = tile_row(to_right)
    copies = []
    for i, old in enumerate((a_ref, b_ref, c_ref)):
        copies.append(
            pltpu.make_async_copy(old.at[pl.ds(right_row, HALO_LOAD)], ahead_buf.at[i, pl.ds(0, HALO_LOAD)], sem.at[2 * i])
        )
        copies.append(
            pltpu.make_async_copy(old.at[pl.ds(0, HALO_LOAD)], behind_buf.at[i, pl.ds(FRONT, HALO_LOAD)], sem.at[2 * i + 1])
        )
    for copy in copies:
        copy.start()
    for i in range(3):
        behind_buf[i, :FRONT, :] = jnp.zeros((FRONT, LANES), jnp.float32)
    for i in range(3):
        copies[2 * i].wait()
        right = shifted(ahead_buf.at[i], to_right - right_row * LANES, HROWS)
        copies[2 * i + 1].wait()
        left = shifted(behind_buf.at[i], to_left + FRONT * LANES, HROWS)
        inner_ref[i] = jnp.where(core == 0, right, left)
        outer_ref[i] = jnp.where(core == 0, left, right)


def own_kernel(bounds_ref, a_ref, b_ref, c_ref, own_ref, buf, sem):
    ahead = lax.axis_index("dp") * P_SIZE - bounds_ref[0]
    row = jnp.maximum(tile_row(ahead), 0)
    copies = []
    for i, old in enumerate((a_ref, b_ref, c_ref)):
        copies.append(
            pltpu.make_async_copy(old.at[pl.ds(pl.multiple_of(row, 8), OWN_LOAD)], buf.at[i, pl.ds(FRONT, OWN_LOAD)], sem.at[i])
        )
    for copy in copies:
        copy.start()
    for i in range(3):
        copies[i].wait()
        own_ref[i] = shifted(buf.at[i], ahead - row * LANES + FRONT * LANES, ROWS)


SEMS = pltpu.SemaphoreType.DMA((6,))
SMEM_SPEC = pl.BlockSpec(memory_space=pltpu.SMEM)
SMALL = pltpu.CompilerParams(vmem_limit_bytes=12 * 1024 * 1024)
ANY_SPEC = pl.BlockSpec(memory_space=pl.ANY)
VMEM_SPEC = pl.BlockSpec(memory_space=pltpu.VMEM)


def halos(bounds, old):
    halo = jax.ShapeDtypeStruct((3, HROWS, LANES), jnp.float32)
    return pl.pallas_call(
        halo_kernel,
        in_specs=[SMEM_SPEC, ANY_SPEC, ANY_SPEC, ANY_SPEC],
        out_specs=(VMEM_SPEC,) * 2,
        out_shape=(halo, halo),
        scratch_shapes=[
            pltpu.VMEM((3, HALO_LOAD + 8, LANES), jnp.float32),
            pltpu.VMEM((3, FRONT + HALO_LOAD, LANES), jnp.float32),
            SEMS,
        ],
        compiler_params=SMALL,
        cost_estimate=pl.CostEstimate(flops=10**6, bytes_accessed=8 * 10**6, transcendentals=0),
    )(bounds, *old)


def own_window(bounds, old):
    return pl.pallas_call(
        own_kernel,
        in_specs=[SMEM_SPEC, ANY_SPEC, ANY_SPEC, ANY_SPEC],
        out_specs=VMEM_SPEC,
        out_shape=jax.ShapeDtypeStruct((3, ROWS, LANES), jnp.float32),
        scratch_shapes=[pltpu.VMEM((3, FRONT + OWN_LOAD + 8, LANES), jnp.float32), SEMS],
        compiler_params=SMALL,
        cost_estimate=pl.CostEstimate(flops=10**6, bytes_accessed=10 * 10**6, transcendentals=0),
    )(bounds, *old)


def adam_kernel(
    bounds_ref, s_ref, t_ref, own_ref, inner_ref, outer_ref, master_ref, first_ref, second_ref, grad, state
):
    row = lax.broadcasted_iota(jnp.int32, (ROWS, LANES), 0)
    lane = lax.broadcasted_iota(jnp.int32, (ROWS, LANES), 1)
    pos = lax.axis_index("dp") * P_SIZE + row * LANES + lane
    tail = ROWS - HROWS
    first_core = lax.bitwise_and(lax.axis_index("dp"), 1) == 0
    below, above = pos[:HROWS] < bounds_ref[0], pos[tail:] >= bounds_ref[1]
    for i in range(3):
        left = jnp.where(first_core, outer_ref[i], inner_ref[i])
        right = jnp.where(first_core, inner_ref[i], outer_ref[i])
        state[i, :HROWS, :] = jnp.where(below, left, own_ref[i, :HROWS, :])
        state[i, HROWS:tail, :] = own_ref[i, HROWS:tail, :]
        state[i, tail:, :] = jnp.where(above, right, own_ref[i, tail:, :])
    tiles = COLS // LANES
    for at in range(16):
        cols = slice(LANES * at, LANES * (at + 1))
        piece = s_ref[:, cols] + t_ref[:, cols]
        for q in range(3):
            grad[pl.ds(16 * q + at, GROWS, stride=tiles), :] = piece[GROWS * q : GROWS * (q + 1)]
        k, c = at // 4, at % 4
        grad[pl.ds(tiles * k + 48 + c, 3, stride=4 * tiles), :] = piece[36:39]
    corr_one = 1.0 - BETA_ONE**ADAM_STEP
    corr_two = 1.0 - BETA_TWO**ADAM_STEP
    g = grad[...]
    first_new = BETA_ONE * state[0] + (1.0 - BETA_ONE) * g
    second_new = BETA_TWO * state[1] + (1.0 - BETA_TWO) * g * g
    master = state[2]
    update = first_new / corr_one / (jnp.sqrt(second_new / corr_two) + EPSILON) + DECAY_RATE * master
    master_ref[...] = master - LEARN_RATE * update
    first_ref[...] = first_new
    second_ref[...] = second_new


def adam_step(bounds, parts, own, left, right):
    shape = jax.ShapeDtypeStruct((ROWS, LANES), jnp.float32)
    return pl.pallas_call(
        adam_kernel,
        in_specs=[SMEM_SPEC] + [VMEM_SPEC] * 5,
        out_specs=(VMEM_SPEC,) * 3,
        out_shape=(shape,) * 3,
        scratch_shapes=[
            pltpu.VMEM((ROWS, LANES), jnp.float32),
            pltpu.VMEM((3, ROWS, LANES), jnp.float32),
        ],
        compiler_params=SMALL,
        cost_estimate=pl.CostEstimate(flops=2 * 10**6, bytes_accessed=3 * 10**6, transcendentals=10**5),
    )(bounds, *parts, own, left, right)


def rep_pairs(move0, move1):
    return [(4 * d + r, 4 * d + (move1 if d % 2 else move0)(r)) for d in range(SHARDS) for r in range(4)]


def local(tokens, cotangent, token_counts, old_bounds, old_first, old_second, old_master):
    bounds = old_bounds.reshape(2)
    old = [a.reshape(CROWS, LANES) for a in (old_first, old_second, old_master)]
    inner, outer = halos(bounds, old)
    own = own_window(bounds, old)
    inner = lax.ppermute(inner, "dp", [(i, i ^ 1) for i in range(SHARDS)])
    outer = lax.ppermute(outer, "dp", [(i, i + 1 if i % 2 else i - 1) for i in range(1, SHARDS - 1)])
    partial = local_gradient(tokens, cotangent, token_counts.reshape(1))
    shard = lax.psum_scatter(partial, "dp", scatter_dimension=0, tiled=True)
    shard = lax.optimization_barrier(shard)
    one, three = (lambda r: r ^ 1), (lambda r: r ^ 3)
    half = shard + lax.ppermute(shard, ("dp", "rep"), rep_pairs(one, three))
    rest = lax.ppermute(half, ("dp", "rep"), rep_pairs(three, one))
    outs = adam_step(bounds, (half, rest), own, inner, outer)
    return tuple(a.reshape(1, P_SIZE) for a in outs)


def solution(mesh):
    placed = (
        P(("dp", "rep"), None),
        P(("dp", "rep"), "mp"),
        P("dp", "rep"),
        P("mp", "dp", None),
        P("mp", "dp"),
        P("mp", "dp"),
        P("mp", "dp"),
    )
    return jax.shard_map(
        local,
        mesh=mesh,
        in_specs=placed,
        out_specs=(P("mp", "dp"), P("mp", "dp"), P("mp", "dp")),
        check_vma=False,
    )
```

```python
import functools

import jax
import jax.numpy as jnp
import numpy as np
from jax import lax
from jax.experimental import pallas as pl
from jax.experimental.pallas import tpu as pltpu
from jax.sharding import PartitionSpec as P

ADAM_STEP = 1000
BETA_ONE = 0.9
BETA_TWO = 0.95
LEARN_RATE = 0.001
DECAY_RATE = 0.1
EPSILON = 1e-08

SHARDS = 24
COLS = 6656
BROWS = 256
LANES = 128
P_SIZE = 79872
HALF = 33280
CAP = 159744
ROWS = P_SIZE // LANES
HROWS = HALF // LANES
CROWS = CAP // LANES
FRONT = 264
SROWS = 39
SCOLS = 2048
STEP_COLS = 512
GROWS = P_SIZE // COLS


def row_class(row):
    return min(row % SROWS // GROWS, 3)


TOTAL = SHARDS * SROWS
TILES_OF = [sorted({row // 8 for row in range(TOTAL) if row_class(row) == c}) for c in range(4)]
PART_ROWS = [(8 * len(tiles) + 15) // 16 * 16 for tiles in TILES_OF]
PART_AT = [sum(PART_ROWS[:c]) for c in range(4)]
PICK_ROWS = sum(PART_ROWS) + 3 * PART_ROWS[3]


def row_picks():
    picks = np.zeros((PICK_ROWS, BROWS), np.float32)
    for c in range(4):
        for i, tile in enumerate(TILES_OF[c]):
            for row in range(8 * tile, 8 * tile + 8):
                if row_class(row) != c:
                    continue
                shard, inner = row // SROWS, row % SROWS
                at = PART_AT[c] + 8 * i + row % 8
                for step in range(4 if c == 3 else 1):
                    token_col = GROWS * shard + (4 * (inner - 36) + step if c == 3 else inner - GROWS * c)
                    if token_col < BROWS:
                        picks[at + step * PART_ROWS[3], token_col] = 1
    return picks.astype(jnp.bfloat16)


def grad_kernel(count_ref, tok_ref, pick_ref, c0_ref, c1_ref, c2_ref, c3_ref, out_ref, lhs_ref, part_ref):
    step = pl.program_id(0)

    @pl.when(step == 0)
    def _():
        tok_row = lax.broadcasted_iota(jnp.int32, (BROWS, BROWS), 0)
        tok = jnp.where(tok_row < count_ref[0], tok_ref[...], jnp.zeros_like(tok_ref))
        lhs_ref[...] = lax.dot_general(
            pick_ref[...], tok, (((1,), (1,)), ((), ())), preferred_element_type=jnp.float32
        ).astype(jnp.bfloat16)

    for c, cot in enumerate((c0_ref, c1_ref, c2_ref, c3_ref)):
        start = PART_AT[c] if c < 3 else pl.multiple_of(PART_AT[3] + step * PART_ROWS[3], 16)
        lhs = lhs_ref[pl.ds(start, PART_ROWS[c]), :]
        part_ref[pl.ds(PART_AT[c], PART_ROWS[c]), :] = jnp.dot(
            lhs, cot[...], preferred_element_type=jnp.float32
        )
    for tile in range(TOTAL // 8):
        found = [PART_AT[c] + 8 * TILES_OF[c].index(tile) for c in range(4) if tile in TILES_OF[c]]
        out_ref[8 * tile : 8 * tile + 8, :] = sum(part_ref[at : at + 8, :] for at in found)


def local_gradient(tokens, cotangent, count):
    block = (BROWS, STEP_COLS)
    return pl.pallas_call(
        grad_kernel,
        grid=(4,),
        in_specs=[
            pl.BlockSpec(memory_space=pltpu.SMEM),
            pl.BlockSpec((BROWS, BROWS), lambda k: (0, 0)),
            pl.BlockSpec((PICK_ROWS, BROWS), lambda k: (0, 0)),
            pl.BlockSpec(block, lambda k: (0, k)),
            pl.BlockSpec(block, lambda k: (0, 4 + k)),
            pl.BlockSpec(block, lambda k: (0, 8 + k)),
            pl.BlockSpec(block, lambda k: (0, 12)),
        ],
        out_specs=pl.BlockSpec((TOTAL, STEP_COLS), lambda k: (0, k)),
        out_shape=jax.ShapeDtypeStruct((TOTAL, SCOLS), jnp.float32),
        scratch_shapes=[
            pltpu.VMEM((PICK_ROWS, BROWS), jnp.bfloat16),
            pltpu.VMEM((sum(PART_ROWS), STEP_COLS), jnp.float32),
        ],
        compiler_params=pltpu.CompilerParams(vmem_limit_bytes=56 * 1024 * 1024),
        cost_estimate=pl.CostEstimate(flops=2 * 10**9, bytes_accessed=12 * 10**6, transcendentals=0),
    )(count, tokens, jnp.asarray(row_picks()), cotangent, cotangent, cotangent, cotangent)


def shifted(ref, start, rows):
    top = lax.shift_right_logical(start, 7)
    lane_start = start - top * LANES
    first = pltpu.roll(ref[pl.ds(top, rows), :], LANES - lane_start, 1)
    second = pltpu.roll(ref[pl.ds(top + 1, rows), :], LANES - lane_start, 1)
    lane = lax.broadcasted_iota(jnp.int32, (rows, LANES), 1)
    return jnp.where(lane < LANES - lane_start, first, second)


HALO_LOAD = HROWS + 12
OWN_LOAD = ROWS + 8


def tile_row(start):
    return pl.multiple_of(lax.shift_left(lax.shift_right_arithmetic(start, 10), 3), 8)


def halo_kernel(
    bounds_ref, a_ref, b_ref, c_ref, inner_hbm, outer_hbm, ahead_buf, behind_buf, inner_ref, outer_ref, sem, out_sem
):
    dp = lax.axis_index("dp")
    core = lax.bitwise_and(dp, 1)
    ahead = dp * P_SIZE - bounds_ref[0]
    to_right, to_left = ahead + P_SIZE, jnp.maximum(ahead, 0) - HALF
    right_row = tile_row(to_right)
    copies = []
    for i, old in enumerate((a_ref, b_ref, c_ref)):
        copies.append(
            pltpu.make_async_copy(old.at[pl.ds(right_row, HALO_LOAD)], ahead_buf.at[i, pl.ds(0, HALO_LOAD)], sem.at[2 * i])
        )
        copies.append(
            pltpu.make_async_copy(old.at[pl.ds(0, HALO_LOAD)], behind_buf.at[i, pl.ds(FRONT, HALO_LOAD)], sem.at[2 * i + 1])
        )
    for copy in copies:
        copy.start()
    for i in range(3):
        behind_buf[i, :FRONT, :] = jnp.zeros((FRONT, LANES), jnp.float32)
    sends = []
    for i in range(3):
        copies[2 * i].wait()
        right = shifted(ahead_buf.at[i], to_right - right_row * LANES, HROWS)
        copies[2 * i + 1].wait()
        left = shifted(behind_buf.at[i], to_left + FRONT * LANES, HROWS)
        inner_ref[i] = jnp.where(core == 0, right, left)
        outer_ref[i] = jnp.where(core == 0, left, right)
        for k, (held, out) in enumerate(((inner_ref, inner_hbm), (outer_ref, outer_hbm))):
            sends.append(pltpu.make_async_copy(held.at[i], out.at[i], out_sem.at[2 * i + k]))
            sends[-1].start()
    for send in sends:
        send.wait()


def own_kernel(bounds_ref, a_ref, b_ref, c_ref, own_ref, buf, sem):
    ahead = lax.axis_index("dp") * P_SIZE - bounds_ref[0]
    row = jnp.maximum(tile_row(ahead), 0)
    copies = []
    for i, old in enumerate((a_ref, b_ref, c_ref)):
        copies.append(
            pltpu.make_async_copy(old.at[pl.ds(pl.multiple_of(row, 8), OWN_LOAD)], buf.at[i, pl.ds(FRONT, OWN_LOAD)], sem.at[i])
        )
    for copy in copies:
        copy.start()
    for i in range(3):
        copies[i].wait()
        own_ref[i] = shifted(buf.at[i], ahead - row * LANES + FRONT * LANES, ROWS)


SEMS = pltpu.SemaphoreType.DMA((6,))
SMEM_SPEC = pl.BlockSpec(memory_space=pltpu.SMEM)
SMALL = pltpu.CompilerParams(vmem_limit_bytes=12 * 1024 * 1024)
ANY_SPEC = pl.BlockSpec(memory_space=pl.ANY)
VMEM_SPEC = pl.BlockSpec(memory_space=pltpu.VMEM)


def halos(bounds, old):
    halo = pltpu.HBM((3, HROWS, LANES), jnp.float32)
    return pl.pallas_call(
        halo_kernel,
        in_specs=[SMEM_SPEC, ANY_SPEC, ANY_SPEC, ANY_SPEC],
        out_specs=(ANY_SPEC,) * 2,
        out_shape=(halo, halo),
        scratch_shapes=[
            pltpu.VMEM((3, HALO_LOAD + 8, LANES), jnp.float32),
            pltpu.VMEM((3, FRONT + HALO_LOAD, LANES), jnp.float32),
            pltpu.VMEM((3, HROWS, LANES), jnp.float32),
            pltpu.VMEM((3, HROWS, LANES), jnp.float32),
            SEMS,
            SEMS,
        ],
        compiler_params=SMALL,
        cost_estimate=pl.CostEstimate(flops=10**6, bytes_accessed=8 * 10**6, transcendentals=0),
    )(bounds, *old)


def own_window(bounds, old):
    return pl.pallas_call(
        own_kernel,
        in_specs=[SMEM_SPEC, ANY_SPEC, ANY_SPEC, ANY_SPEC],
        out_specs=VMEM_SPEC,
        out_shape=jax.ShapeDtypeStruct((3, ROWS, LANES), jnp.float32),
        scratch_shapes=[pltpu.VMEM((3, FRONT + OWN_LOAD + 8, LANES), jnp.float32), SEMS],
        compiler_params=SMALL,
        cost_estimate=pl.CostEstimate(flops=10**6, bytes_accessed=10 * 10**6, transcendentals=0),
    )(bounds, *old)


def adam_kernel(
    bounds_ref, s_ref, t_ref, own_ref, inner_ref, outer_ref, master_ref, first_ref, second_ref, grad, state
):
    row = lax.broadcasted_iota(jnp.int32, (ROWS, LANES), 0)
    lane = lax.broadcasted_iota(jnp.int32, (ROWS, LANES), 1)
    pos = lax.axis_index("dp") * P_SIZE + row * LANES + lane
    tail = ROWS - HROWS
    first_core = lax.bitwise_and(lax.axis_index("dp"), 1) == 0
    below, above = pos[:HROWS] < bounds_ref[0], pos[tail:] >= bounds_ref[1]
    for i in range(3):
        left = jnp.where(first_core, outer_ref[i], inner_ref[i])
        right = jnp.where(first_core, inner_ref[i], outer_ref[i])
        state[i, :HROWS, :] = jnp.where(below, left, own_ref[i, :HROWS, :])
        state[i, HROWS:tail, :] = own_ref[i, HROWS:tail, :]
        state[i, tail:, :] = jnp.where(above, right, own_ref[i, tail:, :])
    tiles = COLS // LANES
    for at in range(16):
        cols = slice(LANES * at, LANES * (at + 1))
        piece = s_ref[:, cols] + t_ref[:, cols]
        for q in range(3):
            grad[pl.ds(16 * q + at, GROWS, stride=tiles), :] = piece[GROWS * q : GROWS * (q + 1)]
        k, c = at // 4, at % 4
        grad[pl.ds(tiles * k + 48 + c, 3, stride=4 * tiles), :] = piece[36:39]
    corr_one = 1.0 - BETA_ONE**ADAM_STEP
    corr_two = 1.0 - BETA_TWO**ADAM_STEP
    g = grad[...]
    first_new = BETA_ONE * state[0] + (1.0 - BETA_ONE) * g
    second_new = BETA_TWO * state[1] + (1.0 - BETA_TWO) * g * g
    master = state[2]
    update = first_new / corr_one / (jnp.sqrt(second_new / corr_two) + EPSILON) + DECAY_RATE * master
    master_ref[...] = master - LEARN_RATE * update
    first_ref[...] = first_new
    second_ref[...] = second_new


def adam_step(bounds, parts, own, left, right):
    shape = jax.ShapeDtypeStruct((ROWS, LANES), jnp.float32)
    return pl.pallas_call(
        adam_kernel,
        in_specs=[SMEM_SPEC] + [VMEM_SPEC] * 5,
        out_specs=(VMEM_SPEC,) * 3,
        out_shape=(shape,) * 3,
        scratch_shapes=[
            pltpu.VMEM((ROWS, LANES), jnp.float32),
            pltpu.VMEM((3, ROWS, LANES), jnp.float32),
        ],
        compiler_params=SMALL,
        cost_estimate=pl.CostEstimate(flops=2 * 10**6, bytes_accessed=3 * 10**6, transcendentals=10**5),
    )(bounds, *parts, own, left, right)


def rep_pairs(move0, move1):
    return [(4 * d + r, 4 * d + (move1 if d % 2 else move0)(r)) for d in range(SHARDS) for r in range(4)]


def local(tokens, cotangent, token_counts, old_bounds, old_first, old_second, old_master):
    bounds = old_bounds.reshape(2)
    old = [a.reshape(CROWS, LANES) for a in (old_first, old_second, old_master)]
    own = own_window(bounds, old)
    partial = local_gradient(tokens, cotangent, token_counts.reshape(1))
    shard = lax.psum_scatter(partial, "dp", scatter_dimension=0, tiled=True)
    shard, inner_out, outer_out = lax.optimization_barrier((shard, *halos(bounds, old)))
    inner = lax.ppermute(inner_out, "dp", [(i, i ^ 1) for i in range(SHARDS)])
    outer = lax.ppermute(outer_out, "dp", [(i, i + 1 if i % 2 else i - 1) for i in range(1, SHARDS - 1)])
    one, three = (lambda r: r ^ 1), (lambda r: r ^ 3)
    half = shard + lax.ppermute(shard, ("dp", "rep"), rep_pairs(one, three))
    rest = lax.ppermute(half, ("dp", "rep"), rep_pairs(three, one))
    outs = adam_step(bounds, (half, rest), own, inner, outer)
    return tuple(a.reshape(1, P_SIZE) for a in outs)


def solution(mesh):
    placed = (
        P(("dp", "rep"), None),
        P(("dp", "rep"), "mp"),
        P("dp", "rep"),
        P("mp", "dp", None),
        P("mp", "dp"),
        P("mp", "dp"),
        P("mp", "dp"),
    )
    return jax.shard_map(
        local,
        mesh=mesh,
        in_specs=placed,
        out_specs=(P("mp", "dp"), P("mp", "dp"), P("mp", "dp")),
        check_vma=False,
    )
```

```python
import functools

import jax
import jax.numpy as jnp
from jax import lax
from jax.experimental import pallas as pl
from jax.experimental.pallas import tpu as pltpu
from jax.sharding import PartitionSpec as P

ADAM_STEP = 1000
BETA_ONE = 0.9
BETA_TWO = 0.95
LEARN_RATE = 0.001
DECAY_RATE = 0.1
EPSILON = 1e-08

SHARDS = 24
COLS = 6656
BROWS = 256
LANES = 128
P_SIZE = 79872
HALF = 33280
CAP = 159744
ROWS = P_SIZE // LANES
HROWS = HALF // LANES
CROWS = CAP // LANES
FRONT = 264
GROWS = P_SIZE // COLS

SMEM_SPEC = pl.BlockSpec(memory_space=pltpu.SMEM)
SMALL = pltpu.CompilerParams(vmem_limit_bytes=12 * 1024 * 1024)
ANY_SPEC = pl.BlockSpec(memory_space=pl.ANY)
HBM_SPEC = pl.BlockSpec(memory_space=pltpu.HBM)
VMEM_SPEC = pl.BlockSpec(memory_space=pltpu.VMEM)
UNIT = 1280
SHARD_COLS = 8 * UNIT
MAIN = COLS
EXTRA = COLS // 2
BLOCKS = 48
PARITY_ROWS = 96


def other(z):
    step = z + 1 if z % 2 else z - 1
    return step % 12


def block_places(chain, core, z, x):
    def side(v):
        w = v + 2 * lax.bitwise_and(v, 1) - 1
        return jnp.where(w < 0, w + 12, jnp.where(w >= 12, w - 12, w))

    def flip(v):
        return lax.bitwise_xor(v, 1)

    xs = later_xs = [x, x ^ 3, x ^ 1, x ^ 2]
    zs = later_zs = [z, side(z), flip(z), side(flip(z))]
    if chain == 1:
        xs = [x, x ^ 1, x ^ 3, x ^ 2]
        zs = [z, flip(z), side(z), flip(side(z))]
    places = []
    for pos in range(BLOCKS):
        a, b, j = pos // 12, (pos % 12) // 3, pos % 3
        x_to = jnp.where(core == 0, xs[a], later_xs[b])
        z_to = jnp.where(core == 0, later_zs[b], zs[a]) + 4 * j
        places.append((jnp.where(z_to >= 12, z_to - 12, z_to), x_to))
    return places


def grad_kernel(count_ref, tok_hbm, cot_hbm, own0_ref, own1_ref, send0_ref, send1_ref, held, tok_ref, cot_ref, sem):
    copies = [pltpu.make_async_copy(tok_hbm, tok_ref, sem.at[0])]
    for i in range(4):
        cols = pl.ds(1664 * i, 1664)
        copies.append(pltpu.make_async_copy(cot_hbm.at[:, cols], cot_ref.at[:, cols], sem.at[1 + i]))
    for copy in copies:
        copy.start()
    dp, x = lax.axis_index("dp"), lax.axis_index("rep")
    z, core = lax.shift_right_logical(dp, 1), lax.bitwise_and(dp, 1)
    copies[0].wait()
    tok_row = lax.broadcasted_iota(jnp.int32, (BROWS, BROWS), 0)
    tok = jnp.where(tok_row < count_ref[0], tok_ref[...], jnp.zeros_like(tok_ref))
    row = lax.broadcasted_iota(jnp.int32, (2 * PARITY_ROWS, BROWS), 0)
    col = lax.broadcasted_iota(jnp.int32, (2 * PARITY_ROWS, BROWS), 1)
    far = row >= PARITY_ROWS
    row = jnp.where(far, row - PARITY_ROWS, row)
    parity = jnp.where(far, 1 - core, core)
    j = lax.bitwise_and(row, 7)
    lead = col - 24 * lax.shift_right_logical(row, 3) - GROWS * parity

    def picked(match):
        one = jnp.where(match, jnp.float32(1), jnp.float32(0)).astype(jnp.bfloat16)
        out = lax.dot_general(one, tok, (((1,), (1,)), ((), ())), preferred_element_type=jnp.float32)
        return out.astype(jnp.bfloat16)

    def dot(a, b):
        return jnp.dot(a, b, preferred_element_type=jnp.float32)

    main = picked(lead == j)
    half_row = lead == 8 + lax.shift_right_logical(j, 1)
    even = picked(half_row & (lax.bitwise_and(j, 1) == 0))
    odd = picked(half_row & (lax.bitwise_and(j, 1) == 1))
    for at in range(0, MAIN, 1664):
        copies[1 + at // 1664].wait()
        held[:, at : at + 1664] = dot(main, cot_ref[:, at : at + 1664])
    for at in range(0, EXTRA, 1664):
        low, high = cot_ref[:, at : at + 1664], cot_ref[:, EXTRA + at : EXTRA + at + 1664]
        held[:, MAIN + at : MAIN + at + 1664] = dot(even, low) + dot(odd, high)
    held[:, MAIN + EXTRA :] = jnp.zeros((2 * PARITY_ROWS, SHARD_COLS - MAIN - EXTRA), jnp.float32)

    for chain, (own, send) in enumerate(((own0_ref, send0_ref), (own1_ref, send1_ref))):
        for far_rows, out, role in ((0, own, core), (PARITY_ROWS, send, 1 - core)):
            for pos, (z_to, x_to) in enumerate(block_places(chain, role, z, x)):
                rows = pl.ds(pl.multiple_of(far_rows + 8 * z_to, 8), 8)
                cols = pl.ds(pl.multiple_of(UNIT * (4 * chain + x_to), LANES), UNIT)
                out[pos] = held[rows, cols]


def local_gradient(tokens, cotangent, count):
    shape = jax.ShapeDtypeStruct((BLOCKS, 8, UNIT), jnp.float32)
    return pl.pallas_call(
        grad_kernel,
        in_specs=[SMEM_SPEC, HBM_SPEC, HBM_SPEC],
        out_specs=(VMEM_SPEC,) * 4,
        out_shape=(shape,) * 4,
        scratch_shapes=[
            pltpu.VMEM((2 * PARITY_ROWS, SHARD_COLS), jnp.float32),
            pltpu.VMEM((BROWS, BROWS), jnp.bfloat16),
            pltpu.VMEM((BROWS, COLS), jnp.bfloat16),
            pltpu.SemaphoreType.DMA((5,)),
        ],
        compiler_params=pltpu.CompilerParams(vmem_limit_bytes=32 * 1024 * 1024),
        cost_estimate=pl.CostEstimate(flops=2 * 10**9, bytes_accessed=11 * 10**6, transcendentals=0),
    )(count, *(pltpu.with_memory_space_constraint(a, pltpu.HBM) for a in (tokens, cotangent)))


def pairs(move0, move1):
    out = []
    for dp in range(SHARDS):
        for x in range(4):
            z, core = dp // 2, dp % 2
            z_to, x_to = (move1 if core else move0)(z, x)
            out.append((4 * dp + x, 4 * (2 * z_to + core) + x_to))
    return out


def reduced(own, send, bounds, old):
    def x1(z, x):
        return z, x ^ 1

    def x2(z, x):
        return z, x ^ 2

    def x3(z, x):
        return z, x ^ 3

    def z1(z, x):
        return z ^ 1, x

    def zo(z, x):
        return other(z), x

    def zt(z, x):
        return other(z ^ 1), x

    axes = ("dp", "rep")
    first, second = ((x1, z1), (x3, zo)), ((x3, zo), (x1, z1))
    swap = [(i, i ^ 1) for i in range(SHARDS)]
    held = []
    for c in range(2):
        got = lax.ppermute(send[c], "dp", swap)
        far = lax.ppermute(own[c][24:] + got[24:], axes, pairs(*first[c]))
        held.append([own[c][i : i + 12] + got[i : i + 12] + far[i : i + 12] for i in (0, 12)])
        if c == 0:
            inner, outer, state = windows(bounds, old)
            *held[0], inner, outer, state = lax.optimization_barrier((*held[0], inner, outer, state))
    held = [held[c][0] + lax.ppermute(held[c][1], axes, pairs(*second[c])) for c in range(2)]
    got = [
        lax.ppermute(jnp.stack([h[3 * i : 3 * i + 3] for h in held]), axes, pairs(*to))
        for i, to in ((1, (zo, x3)), (2, (z1, x1)), (3, (zt, x2)))
    ]
    rest = [
        jnp.stack([h[i] for h in held]) + got[0][:, i] + got[1][:, i] + got[2][:, i] for i in range(3)
    ]
    *rest, inner, outer = lax.optimization_barrier((*rest, inner, outer))
    inner = lax.ppermute(inner, "dp", swap)
    outer = lax.ppermute(outer, "dp", [(i, i + 1 if i % 2 else i - 1) for i in range(1, SHARDS - 1)])
    ahead = [(i, (i + 8) % SHARDS) for i in range(SHARDS)]
    behind = [(i, (i - 8) % SHARDS) for i in range(SHARDS)]
    mine = rest[0] + lax.ppermute(rest[1], "dp", ahead) + lax.ppermute(rest[2], "dp", behind)
    return lax.all_gather(mine, "rep", axis=0, tiled=False), (state, inner, outer)


def shifted(ref, start, rows):
    start = start + FRONT * LANES
    top = lax.shift_right_logical(start, 7)
    lane_start = start - top * LANES
    first = pltpu.roll(ref[pl.ds(top, rows), :], LANES - lane_start, 1)
    second = pltpu.roll(ref[pl.ds(top + 1, rows), :], LANES - lane_start, 1)
    lane = lax.broadcasted_iota(jnp.int32, (rows, LANES), 1)
    return jnp.where(lane < LANES - lane_start, first, second)


def load_old(refs, buf, sem):
    copies = [pltpu.make_async_copy(r, buf.at[i, pl.ds(FRONT, CROWS)], sem.at[i]) for i, r in enumerate(refs)]
    for c in copies:
        c.start()
    for i in range(3):
        buf[i, :FRONT, :] = jnp.zeros((FRONT, LANES), jnp.float32)
        buf[i, FRONT + CROWS :, :] = jnp.zeros((8, LANES), jnp.float32)
    for c in copies:
        c.wait()


def window_kernel(bounds_ref, a_ref, b_ref, c_ref, inner_ref, outer_ref, own_ref, buf, sem):
    load_old((a_ref, b_ref, c_ref), buf, sem)
    dp = lax.axis_index("dp")
    core = lax.bitwise_and(dp, 1)
    ahead = dp * P_SIZE - bounds_ref[0]
    to_right, to_left = ahead + P_SIZE, jnp.maximum(ahead, 0) - HALF
    for i in range(3):
        inner_ref[i] = shifted(buf.at[i], jnp.where(core == 0, to_right, to_left), HROWS)
        outer_ref[i] = shifted(buf.at[i], jnp.where(core == 0, to_left, to_right), HROWS)
        own_ref[i] = shifted(buf.at[i], ahead, ROWS)


OLD_SCRATCH = (
    pltpu.VMEM((3, FRONT + CROWS + 8, LANES), jnp.float32),
    pltpu.SemaphoreType.DMA((3,)),
)


def windows(bounds, old):
    halo = jax.ShapeDtypeStruct((3, HROWS, LANES), jnp.float32)
    own = jax.ShapeDtypeStruct((3, ROWS, LANES), jnp.float32)
    return pl.pallas_call(
        window_kernel,
        in_specs=[SMEM_SPEC, ANY_SPEC, ANY_SPEC, ANY_SPEC],
        out_specs=(VMEM_SPEC,) * 3,
        out_shape=(halo, halo, own),
        scratch_shapes=list(OLD_SCRATCH),
        compiler_params=SMALL,
        cost_estimate=pl.CostEstimate(flops=10**6, bytes_accessed=16 * 10**6, transcendentals=0),
    )(bounds, *old)


def adam_kernel(
    bounds_ref, parts_ref, own_ref, inner_ref, outer_ref,
    master_ref, first_ref, second_ref, shard, grad, state,
):
    row = lax.broadcasted_iota(jnp.int32, (ROWS, LANES), 0)
    lane = lax.broadcasted_iota(jnp.int32, (ROWS, LANES), 1)
    pos = lax.axis_index("dp") * P_SIZE + row * LANES + lane
    tail = ROWS - HROWS
    first_core = lax.bitwise_and(lax.axis_index("dp"), 1) == 0
    below, above = pos[:HROWS] < bounds_ref[0], pos[tail:] >= bounds_ref[1]
    for i in range(3):
        left = jnp.where(first_core, outer_ref[i], inner_ref[i])
        right = jnp.where(first_core, inner_ref[i], outer_ref[i])
        state[i, :HROWS, :] = jnp.where(below, left, own_ref[i, :HROWS, :])
        state[i, HROWS:tail, :] = own_ref[i, HROWS:tail, :]
        state[i, tail:, :] = jnp.where(above, right, own_ref[i, tail:, :])
    for place in range(4):
        for chain in range(2):
            at = UNIT * (4 * chain + place)
            shard[:, at : at + UNIT] = parts_ref[place, chain]
    tiles = COLS // LANES
    for at in range(tiles):
        grad[pl.ds(at, 8, stride=tiles), :] = shard[:, LANES * at : LANES * (at + 1)]
    for at in range(tiles // 2):
        col = MAIN + LANES * at
        grad[pl.ds(8 * tiles + at, 8, stride=tiles // 2), :] = shard[:, col : col + LANES]
    corr_one = 1.0 - BETA_ONE**ADAM_STEP
    corr_two = 1.0 - BETA_TWO**ADAM_STEP
    g = grad[...]
    first_new = BETA_ONE * state[0] + (1.0 - BETA_ONE) * g
    second_new = BETA_TWO * state[1] + (1.0 - BETA_TWO) * g * g
    master = state[2]
    update = first_new / corr_one / (jnp.sqrt(second_new / corr_two) + EPSILON) + DECAY_RATE * master
    master_ref[...] = master - LEARN_RATE * update
    first_ref[...] = first_new
    second_ref[...] = second_new


def adam_step(bounds, parts, own, left, right):
    shape = jax.ShapeDtypeStruct((ROWS, LANES), jnp.float32)
    return pl.pallas_call(
        adam_kernel,
        in_specs=[SMEM_SPEC] + [VMEM_SPEC] * 4,
        out_specs=(VMEM_SPEC,) * 3,
        out_shape=(shape,) * 3,
        scratch_shapes=[
            pltpu.VMEM((8, SHARD_COLS), jnp.float32),
            pltpu.VMEM((ROWS, LANES), jnp.float32),
            pltpu.VMEM((3, ROWS, LANES), jnp.float32),
        ],
        compiler_params=SMALL,
        cost_estimate=pl.CostEstimate(flops=2 * 10**6, bytes_accessed=3 * 10**6, transcendentals=10**5),
    )(bounds, parts, own, left, right)


def local(tokens, cotangent, token_counts, old_bounds, old_first, old_second, old_master):
    bounds = old_bounds.reshape(2)
    old = [a.reshape(CROWS, LANES) for a in (old_first, old_second, old_master)]
    own0, own1, send0, send1 = local_gradient(tokens, cotangent, token_counts.reshape(1))
    parts, state = reduced((own0, own1), (send0, send1), bounds, old)
    outs = adam_step(bounds, parts, *state)
    return tuple(a.reshape(1, P_SIZE) for a in outs)


def solution(mesh):
    placed = (
        P(("dp", "rep"), None),
        P(("dp", "rep"), "mp"),
        P("dp", "rep"),
        P("mp", "dp", None),
        P("mp", "dp"),
        P("mp", "dp"),
        P("mp", "dp"),
    )
    return jax.shard_map(
        local,
        mesh=mesh,
        in_specs=placed,
        out_specs=(P("mp", "dp"), P("mp", "dp"), P("mp", "dp")),
        check_vma=False,
    )
```

```python
import functools

import jax
import jax.numpy as jnp
from jax import lax
from jax.experimental import pallas as pl
from jax.experimental.pallas import tpu as pltpu
from jax.sharding import PartitionSpec as P

ADAM_STEP = 1000
BETA_ONE = 0.9
BETA_TWO = 0.95
LEARN_RATE = 0.001
DECAY_RATE = 0.1
EPSILON = 1e-08

SHARDS = 24
COLS = 6656
BROWS = 256
LANES = 128
P_SIZE = 79872
HALF = 33280
CAP = 159744
ROWS = P_SIZE // LANES
HROWS = HALF // LANES
CROWS = CAP // LANES
FRONT = 264
GROWS = P_SIZE // COLS

SMEM_SPEC = pl.BlockSpec(memory_space=pltpu.SMEM)
SMALL = pltpu.CompilerParams(vmem_limit_bytes=12 * 1024 * 1024)
ANY_SPEC = pl.BlockSpec(memory_space=pl.ANY)
HBM_SPEC = pl.BlockSpec(memory_space=pltpu.HBM)
VMEM_SPEC = pl.BlockSpec(memory_space=pltpu.VMEM)
UNIT = 1280
SHARD_COLS = 8 * UNIT
MAIN = COLS
EXTRA = COLS // 2
BLOCKS = 48
PARITY_ROWS = 96


def other(z):
    step = z + 1 if z % 2 else z - 1
    return step % 12


def block_places(chain, core, z, x):
    def side(v):
        w = v + 2 * lax.bitwise_and(v, 1) - 1
        return jnp.where(w < 0, w + 12, jnp.where(w >= 12, w - 12, w))

    def flip(v):
        return lax.bitwise_xor(v, 1)

    xs = later_xs = [x, x ^ 3, x ^ 1, x ^ 2]
    zs = later_zs = [z, side(z), flip(z), side(flip(z))]
    if chain == 1:
        xs = [x, x ^ 1, x ^ 3, x ^ 2]
        zs = [z, flip(z), side(z), flip(side(z))]
    places = []
    for pos in range(BLOCKS):
        a, b, j = pos // 12, (pos % 12) // 3, pos % 3
        x_to = jnp.where(core == 0, xs[a], later_xs[b])
        z_to = jnp.where(core == 0, later_zs[b], zs[a]) + 4 * j
        places.append((jnp.where(z_to >= 12, z_to - 12, z_to), x_to))
    return places


def grad_kernel(count_ref, tok_hbm, cot_hbm, own0_ref, own1_ref, send0_ref, send1_ref, held, tok_ref, cot_ref, sem):
    copies = [pltpu.make_async_copy(tok_hbm, tok_ref, sem.at[0])]
    for i in range(4):
        cols = pl.ds(1664 * i, 1664)
        copies.append(pltpu.make_async_copy(cot_hbm.at[:, cols], cot_ref.at[:, cols], sem.at[1 + i]))
    for copy in copies:
        copy.start()
    dp, x = lax.axis_index("dp"), lax.axis_index("rep")
    z, core = lax.shift_right_logical(dp, 1), lax.bitwise_and(dp, 1)
    copies[0].wait()
    tok_row = lax.broadcasted_iota(jnp.int32, (BROWS, BROWS), 0)
    tok = jnp.where(tok_row < count_ref[0], tok_ref[...], jnp.zeros_like(tok_ref))
    row = lax.broadcasted_iota(jnp.int32, (2 * PARITY_ROWS, BROWS), 0)
    col = lax.broadcasted_iota(jnp.int32, (2 * PARITY_ROWS, BROWS), 1)
    far = row >= PARITY_ROWS
    row = jnp.where(far, row - PARITY_ROWS, row)
    parity = jnp.where(far, 1 - core, core)
    j = lax.bitwise_and(row, 7)
    lead = col - 24 * lax.shift_right_logical(row, 3) - GROWS * parity

    def picked(match):
        one = jnp.where(match, jnp.float32(1), jnp.float32(0)).astype(jnp.bfloat16)
        out = lax.dot_general(one, tok, (((1,), (1,)), ((), ())), preferred_element_type=jnp.float32)
        return out.astype(jnp.bfloat16)

    def dot(a, b):
        return jnp.dot(a, b, preferred_element_type=jnp.float32)

    main = picked(lead == j)
    half_row = lead == 8 + lax.shift_right_logical(j, 1)
    even = picked(half_row & (lax.bitwise_and(j, 1) == 0))
    odd = picked(half_row & (lax.bitwise_and(j, 1) == 1))
    for at in range(0, MAIN, 1664):
        copies[1 + at // 1664].wait()
        held[:, at : at + 1664] = dot(main, cot_ref[:, at : at + 1664])
    for at in range(0, EXTRA, 1664):
        low, high = cot_ref[:, at : at + 1664], cot_ref[:, EXTRA + at : EXTRA + at + 1664]
        held[:, MAIN + at : MAIN + at + 1664] = dot(even, low) + dot(odd, high)
    held[:, MAIN + EXTRA :] = jnp.zeros((2 * PARITY_ROWS, SHARD_COLS - MAIN - EXTRA), jnp.float32)

    for chain, (own, send) in enumerate(((own0_ref, send0_ref), (own1_ref, send1_ref))):
        for far_rows, out, role in ((0, own, core), (PARITY_ROWS, send, 1 - core)):
            for pos, (z_to, x_to) in enumerate(block_places(chain, role, z, x)):
                rows = pl.ds(pl.multiple_of(far_rows + 8 * z_to, 8), 8)
                cols = pl.ds(pl.multiple_of(UNIT * (4 * chain + x_to), LANES), UNIT)
                out[pos] = held[rows, cols]


def local_gradient(tokens, cotangent, count):
    shape = jax.ShapeDtypeStruct((BLOCKS, 8, UNIT), jnp.float32)
    return pl.pallas_call(
        grad_kernel,
        in_specs=[SMEM_SPEC, HBM_SPEC, HBM_SPEC],
        out_specs=(VMEM_SPEC,) * 4,
        out_shape=(shape,) * 4,
        scratch_shapes=[
            pltpu.VMEM((2 * PARITY_ROWS, SHARD_COLS), jnp.float32),
            pltpu.VMEM((BROWS, BROWS), jnp.bfloat16),
            pltpu.VMEM((BROWS, COLS), jnp.bfloat16),
            pltpu.SemaphoreType.DMA((5,)),
        ],
        compiler_params=pltpu.CompilerParams(vmem_limit_bytes=32 * 1024 * 1024),
        cost_estimate=pl.CostEstimate(flops=2 * 10**9, bytes_accessed=11 * 10**6, transcendentals=0),
    )(count, *(pltpu.with_memory_space_constraint(a, pltpu.HBM) for a in (tokens, cotangent)))


def pairs(move0, move1):
    out = []
    for dp in range(SHARDS):
        for x in range(4):
            z, core = dp // 2, dp % 2
            z_to, x_to = (move1 if core else move0)(z, x)
            out.append((4 * dp + x, 4 * (2 * z_to + core) + x_to))
    return out


def reduced(own, send, bounds, old):
    def x1(z, x):
        return z, x ^ 1

    def x2(z, x):
        return z, x ^ 2

    def x3(z, x):
        return z, x ^ 3

    def z1(z, x):
        return z ^ 1, x

    def zo(z, x):
        return other(z), x

    def zt(z, x):
        return other(z ^ 1), x

    axes = ("dp", "rep")
    first, second = ((x1, z1), (x3, zo)), ((x3, zo), (x1, z1))
    swap = [(i, i ^ 1) for i in range(SHARDS)]
    held = []
    for c in range(2):
        got = lax.ppermute(send[c], "dp", swap)
        far = lax.ppermute(own[c][24:] + got[24:], axes, pairs(*first[c]))
        held.append([own[c][i : i + 12] + got[i : i + 12] + far[i : i + 12] for i in (0, 12)])
        if c == 0:
            inner, outer, state = windows(bounds, old)
            inner = lax.ppermute(inner, "dp", swap)
            *held[0], outer, state = lax.optimization_barrier((*held[0], outer, state))
    *held[1], inner = lax.optimization_barrier((*held[1], inner))
    held = [held[c][0] + lax.ppermute(held[c][1], axes, pairs(*second[c])) for c in range(2)]
    got = [
        lax.ppermute(jnp.stack([h[3 * i : 3 * i + 3] for h in held]), axes, pairs(*to))
        for i, to in ((1, (zo, x3)), (2, (z1, x1)), (3, (zt, x2)))
    ]
    rest = [
        jnp.stack([h[i] for h in held]) + got[0][:, i] + got[1][:, i] + got[2][:, i] for i in range(3)
    ]
    *rest, outer = lax.optimization_barrier((*rest, outer))
    outer = lax.ppermute(outer, "dp", [(i, i + 1 if i % 2 else i - 1) for i in range(1, SHARDS - 1)])
    ahead = [(i, (i + 8) % SHARDS) for i in range(SHARDS)]
    behind = [(i, (i - 8) % SHARDS) for i in range(SHARDS)]
    mine = rest[0] + lax.ppermute(rest[1], "dp", ahead) + lax.ppermute(rest[2], "dp", behind)
    return lax.all_gather(mine, "rep", axis=0, tiled=False), (state, inner, outer)


def shifted(ref, start, rows):
    start = start + FRONT * LANES
    top = lax.shift_right_logical(start, 7)
    lane_start = start - top * LANES
    first = pltpu.roll(ref[pl.ds(top, rows), :], LANES - lane_start, 1)
    second = pltpu.roll(ref[pl.ds(top + 1, rows), :], LANES - lane_start, 1)
    lane = lax.broadcasted_iota(jnp.int32, (rows, LANES), 1)
    return jnp.where(lane < LANES - lane_start, first, second)


def load_old(refs, buf, sem):
    copies = [pltpu.make_async_copy(r, buf.at[i, pl.ds(FRONT, CROWS)], sem.at[i]) for i, r in enumerate(refs)]
    for c in copies:
        c.start()
    for i in range(3):
        buf[i, :FRONT, :] = jnp.zeros((FRONT, LANES), jnp.float32)
        buf[i, FRONT + CROWS :, :] = jnp.zeros((8, LANES), jnp.float32)
    for c in copies:
        c.wait()


def window_kernel(bounds_ref, a_ref, b_ref, c_ref, inner_ref, outer_ref, own_ref, buf, sem):
    load_old((a_ref, b_ref, c_ref), buf, sem)
    dp = lax.axis_index("dp")
    core = lax.bitwise_and(dp, 1)
    ahead = dp * P_SIZE - bounds_ref[0]
    to_right, to_left = ahead + P_SIZE, jnp.maximum(ahead, 0) - HALF
    for i in range(3):
        inner_ref[i] = shifted(buf.at[i], jnp.where(core == 0, to_right, to_left), HROWS)
        outer_ref[i] = shifted(buf.at[i], jnp.where(core == 0, to_left, to_right), HROWS)
        own_ref[i] = shifted(buf.at[i], ahead, ROWS)


OLD_SCRATCH = (
    pltpu.VMEM((3, FRONT + CROWS + 8, LANES), jnp.float32),
    pltpu.SemaphoreType.DMA((3,)),
)


def windows(bounds, old):
    halo = jax.ShapeDtypeStruct((3, HROWS, LANES), jnp.float32)
    own = jax.ShapeDtypeStruct((3, ROWS, LANES), jnp.float32)
    return pl.pallas_call(
        window_kernel,
        in_specs=[SMEM_SPEC, ANY_SPEC, ANY_SPEC, ANY_SPEC],
        out_specs=(VMEM_SPEC,) * 3,
        out_shape=(halo, halo, own),
        scratch_shapes=list(OLD_SCRATCH),
        compiler_params=SMALL,
        cost_estimate=pl.CostEstimate(flops=10**6, bytes_accessed=16 * 10**6, transcendentals=0),
    )(bounds, *old)


def adam_kernel(
    bounds_ref, parts_ref, own_ref, inner_ref, outer_ref,
    master_ref, first_ref, second_ref, shard, grad, state,
):
    row = lax.broadcasted_iota(jnp.int32, (ROWS, LANES), 0)
    lane = lax.broadcasted_iota(jnp.int32, (ROWS, LANES), 1)
    pos = lax.axis_index("dp") * P_SIZE + row * LANES + lane
    tail = ROWS - HROWS
    first_core = lax.bitwise_and(lax.axis_index("dp"), 1) == 0
    below, above = pos[:HROWS] < bounds_ref[0], pos[tail:] >= bounds_ref[1]
    for i in range(3):
        left = jnp.where(first_core, outer_ref[i], inner_ref[i])
        right = jnp.where(first_core, inner_ref[i], outer_ref[i])
        state[i, :HROWS, :] = jnp.where(below, left, own_ref[i, :HROWS, :])
        state[i, HROWS:tail, :] = own_ref[i, HROWS:tail, :]
        state[i, tail:, :] = jnp.where(above, right, own_ref[i, tail:, :])
    for place in range(4):
        for chain in range(2):
            at = UNIT * (4 * chain + place)
            shard[:, at : at + UNIT] = parts_ref[place, chain]
    tiles = COLS // LANES
    for at in range(tiles):
        grad[pl.ds(at, 8, stride=tiles), :] = shard[:, LANES * at : LANES * (at + 1)]
    for at in range(tiles // 2):
        col = MAIN + LANES * at
        grad[pl.ds(8 * tiles + at, 8, stride=tiles // 2), :] = shard[:, col : col + LANES]
    corr_one = 1.0 - BETA_ONE**ADAM_STEP
    corr_two = 1.0 - BETA_TWO**ADAM_STEP
    g = grad[...]
    first_new = BETA_ONE * state[0] + (1.0 - BETA_ONE) * g
    second_new = BETA_TWO * state[1] + (1.0 - BETA_TWO) * g * g
    master = state[2]
    update = first_new / corr_one / (jnp.sqrt(second_new / corr_two) + EPSILON) + DECAY_RATE * master
    master_ref[...] = master - LEARN_RATE * update
    first_ref[...] = first_new
    second_ref[...] = second_new


def adam_step(bounds, parts, own, left, right):
    shape = jax.ShapeDtypeStruct((ROWS, LANES), jnp.float32)
    return pl.pallas_call(
        adam_kernel,
        in_specs=[SMEM_SPEC] + [VMEM_SPEC] * 4,
        out_specs=(VMEM_SPEC,) * 3,
        out_shape=(shape,) * 3,
        scratch_shapes=[
            pltpu.VMEM((8, SHARD_COLS), jnp.float32),
            pltpu.VMEM((ROWS, LANES), jnp.float32),
            pltpu.VMEM((3, ROWS, LANES), jnp.float32),
        ],
        compiler_params=SMALL,
        cost_estimate=pl.CostEstimate(flops=2 * 10**6, bytes_accessed=3 * 10**6, transcendentals=10**5),
    )(bounds, parts, own, left, right)


def local(tokens, cotangent, token_counts, old_bounds, old_first, old_second, old_master):
    bounds = old_bounds.reshape(2)
    old = [a.reshape(CROWS, LANES) for a in (old_first, old_second, old_master)]
    own0, own1, send0, send1 = local_gradient(tokens, cotangent, token_counts.reshape(1))
    parts, state = reduced((own0, own1), (send0, send1), bounds, old)
    outs = adam_step(bounds, parts, *state)
    return tuple(a.reshape(1, P_SIZE) for a in outs)


def solution(mesh):
    placed = (
        P(("dp", "rep"), None),
        P(("dp", "rep"), "mp"),
        P("dp", "rep"),
        P("mp", "dp", None),
        P("mp", "dp"),
        P("mp", "dp"),
        P("mp", "dp"),
    )
    return jax.shard_map(
        local,
        mesh=mesh,
        in_specs=placed,
        out_specs=(P("mp", "dp"), P("mp", "dp"), P("mp", "dp")),
        check_vma=False,
    )
```

```python
import functools

import jax
import jax.numpy as jnp
from jax import lax
from jax.experimental import pallas as pl
from jax.experimental.pallas import tpu as pltpu
from jax.sharding import PartitionSpec as P

ADAM_STEP = 1000
BETA_ONE = 0.9
BETA_TWO = 0.95
LEARN_RATE = 0.001
DECAY_RATE = 0.1
EPSILON = 1e-08

SHARDS = 24
COLS = 6656
BROWS = 256
LANES = 128
P_SIZE = 79872
HALF = 33280
CAP = 159744
ROWS = P_SIZE // LANES
HROWS = HALF // LANES
CROWS = CAP // LANES
FRONT = 264
GROWS = P_SIZE // COLS

SMEM_SPEC = pl.BlockSpec(memory_space=pltpu.SMEM)
SMALL = pltpu.CompilerParams(vmem_limit_bytes=12 * 1024 * 1024)
ANY_SPEC = pl.BlockSpec(memory_space=pl.ANY)
HBM_SPEC = pl.BlockSpec(memory_space=pltpu.HBM)
VMEM_SPEC = pl.BlockSpec(memory_space=pltpu.VMEM)
UNIT = 1280
SHARD_COLS = 8 * UNIT
MAIN = COLS
EXTRA = COLS // 2
BLOCKS = 48
PARITY_ROWS = 96


def other(z):
    step = z + 1 if z % 2 else z - 1
    return step % 12


def block_places(chain, core, z, x):
    def side(v):
        w = v + 2 * lax.bitwise_and(v, 1) - 1
        return jnp.where(w < 0, w + 12, jnp.where(w >= 12, w - 12, w))

    def flip(v):
        return lax.bitwise_xor(v, 1)

    xs = later_xs = [x, x ^ 3, x ^ 1, x ^ 2]
    zs = later_zs = [z, side(z), flip(z), side(flip(z))]
    if chain == 1:
        xs = [x, x ^ 1, x ^ 3, x ^ 2]
        zs = [z, flip(z), side(z), flip(side(z))]
    places = []
    for pos in range(BLOCKS):
        a, b, j = pos // 12, (pos % 12) // 3, pos % 3
        x_to = jnp.where(core == 0, xs[a], later_xs[b])
        z_to = jnp.where(core == 0, later_zs[b], zs[a]) + 4 * j
        places.append((jnp.where(z_to >= 12, z_to - 12, z_to), x_to))
    return places


def grad_kernel(count_ref, tok_hbm, cot_hbm, own0_ref, own1_ref, send0_ref, send1_ref, held, tok_ref, cot_ref, sem):
    copies = [pltpu.make_async_copy(tok_hbm, tok_ref, sem.at[0])]
    for i in range(4):
        cols = pl.ds(1664 * i, 1664)
        copies.append(pltpu.make_async_copy(cot_hbm.at[:, cols], cot_ref.at[:, cols], sem.at[1 + i]))
    for copy in copies:
        copy.start()
    dp, x = lax.axis_index("dp"), lax.axis_index("rep")
    z, core = lax.shift_right_logical(dp, 1), lax.bitwise_and(dp, 1)
    copies[0].wait()
    tok_row = lax.broadcasted_iota(jnp.int32, (BROWS, BROWS), 0)
    tok = jnp.where(tok_row < count_ref[0], tok_ref[...], jnp.zeros_like(tok_ref))
    row = lax.broadcasted_iota(jnp.int32, (2 * PARITY_ROWS, BROWS), 0)
    col = lax.broadcasted_iota(jnp.int32, (2 * PARITY_ROWS, BROWS), 1)
    far = row >= PARITY_ROWS
    row = jnp.where(far, row - PARITY_ROWS, row)
    parity = jnp.where(far, 1 - core, core)
    j = lax.bitwise_and(row, 7)
    lead = col - 24 * lax.shift_right_logical(row, 3) - GROWS * parity

    def picked(match):
        one = jnp.where(match, jnp.float32(1), jnp.float32(0)).astype(jnp.bfloat16)
        out = lax.dot_general(one, tok, (((1,), (1,)), ((), ())), preferred_element_type=jnp.float32)
        return out.astype(jnp.bfloat16)

    def dot(a, b):
        return jnp.dot(a, b, preferred_element_type=jnp.float32)

    main = picked(lead == j)
    half_row = lead == 8 + lax.shift_right_logical(j, 1)
    even = picked(half_row & (lax.bitwise_and(j, 1) == 0))
    odd = picked(half_row & (lax.bitwise_and(j, 1) == 1))
    for at in range(0, MAIN, 1664):
        copies[1 + at // 1664].wait()
        held[:, at : at + 1664] = dot(main, cot_ref[:, at : at + 1664])
    for at in range(0, EXTRA, 1664):
        low, high = cot_ref[:, at : at + 1664], cot_ref[:, EXTRA + at : EXTRA + at + 1664]
        held[:, MAIN + at : MAIN + at + 1664] = dot(even, low) + dot(odd, high)
    held[:, MAIN + EXTRA :] = jnp.zeros((2 * PARITY_ROWS, SHARD_COLS - MAIN - EXTRA), jnp.float32)

    for chain, (own, send) in enumerate(((own0_ref, send0_ref), (own1_ref, send1_ref))):
        for far_rows, out, role in ((0, own, core), (PARITY_ROWS, send, 1 - core)):
            for pos, (z_to, x_to) in enumerate(block_places(chain, role, z, x)):
                rows = pl.ds(pl.multiple_of(far_rows + 8 * z_to, 8), 8)
                cols = pl.ds(pl.multiple_of(UNIT * (4 * chain + x_to), LANES), UNIT)
                out[pos] = held[rows, cols]


def local_gradient(tokens, cotangent, count):
    shape = jax.ShapeDtypeStruct((BLOCKS, 8, UNIT), jnp.float32)
    return pl.pallas_call(
        grad_kernel,
        in_specs=[SMEM_SPEC, HBM_SPEC, HBM_SPEC],
        out_specs=(VMEM_SPEC,) * 4,
        out_shape=(shape,) * 4,
        scratch_shapes=[
            pltpu.VMEM((2 * PARITY_ROWS, SHARD_COLS), jnp.float32),
            pltpu.VMEM((BROWS, BROWS), jnp.bfloat16),
            pltpu.VMEM((BROWS, COLS), jnp.bfloat16),
            pltpu.SemaphoreType.DMA((5,)),
        ],
        compiler_params=pltpu.CompilerParams(vmem_limit_bytes=32 * 1024 * 1024),
        cost_estimate=pl.CostEstimate(flops=2 * 10**9, bytes_accessed=11 * 10**6, transcendentals=0),
    )(count, *(pltpu.with_memory_space_constraint(a, pltpu.HBM) for a in (tokens, cotangent)))


def pairs(move0, move1):
    out = []
    for dp in range(SHARDS):
        for x in range(4):
            z, core = dp // 2, dp % 2
            z_to, x_to = (move1 if core else move0)(z, x)
            out.append((4 * dp + x, 4 * (2 * z_to + core) + x_to))
    return out


def reduced(own, send, bounds, old):
    def x1(z, x):
        return z, x ^ 1

    def x2(z, x):
        return z, x ^ 2

    def x3(z, x):
        return z, x ^ 3

    def z1(z, x):
        return z ^ 1, x

    def zo(z, x):
        return other(z), x

    def zt(z, x):
        return other(z ^ 1), x

    axes = ("dp", "rep")
    first, second = ((x1, z1), (x3, zo)), ((x3, zo), (x1, z1))
    swap = [(i, i ^ 1) for i in range(SHARDS)]
    held = []
    for c in range(2):
        got = lax.ppermute(send[c], "dp", swap)
        far = lax.ppermute(own[c][24:] + got[24:], axes, pairs(*first[c]))
        held.append([own[c][i : i + 12] + got[i : i + 12] + far[i : i + 12] for i in (0, 12)])
        if c == 0:
            inner, outer, state = windows(bounds, old)
            inner = lax.ppermute(inner, "dp", swap)
            outer = lax.ppermute(outer, "dp", [(i, i + 1 if i % 2 else i - 1) for i in range(1, SHARDS - 1)])
            *held[0], state = lax.optimization_barrier((*held[0], state))
    *held[1], inner, outer = lax.optimization_barrier((*held[1], inner, outer))
    held = [held[c][0] + lax.ppermute(held[c][1], axes, pairs(*second[c])) for c in range(2)]
    got = [
        lax.ppermute(jnp.stack([h[3 * i : 3 * i + 3] for h in held]), axes, pairs(*to))
        for i, to in ((1, (zo, x3)), (2, (z1, x1)), (3, (zt, x2)))
    ]
    rest = [
        jnp.stack([h[i] for h in held]) + got[0][:, i] + got[1][:, i] + got[2][:, i] for i in range(3)
    ]
    ahead = [(i, (i + 8) % SHARDS) for i in range(SHARDS)]
    behind = [(i, (i - 8) % SHARDS) for i in range(SHARDS)]
    mine = rest[0] + lax.ppermute(rest[1], "dp", ahead) + lax.ppermute(rest[2], "dp", behind)
    return lax.all_gather(mine, "rep", axis=0, tiled=False), (state, inner, outer)


def shifted(ref, start, rows):
    start = start + FRONT * LANES
    top = lax.shift_right_logical(start, 7)
    lane_start = start - top * LANES
    first = pltpu.roll(ref[pl.ds(top, rows), :], LANES - lane_start, 1)
    second = pltpu.roll(ref[pl.ds(top + 1, rows), :], LANES - lane_start, 1)
    lane = lax.broadcasted_iota(jnp.int32, (rows, LANES), 1)
    return jnp.where(lane < LANES - lane_start, first, second)


def load_old(refs, buf, sem):
    copies = [pltpu.make_async_copy(r, buf.at[i, pl.ds(FRONT, CROWS)], sem.at[i]) for i, r in enumerate(refs)]
    for c in copies:
        c.start()
    for i in range(3):
        buf[i, :FRONT, :] = jnp.zeros((FRONT, LANES), jnp.float32)
        buf[i, FRONT + CROWS :, :] = jnp.zeros((8, LANES), jnp.float32)
    for c in copies:
        c.wait()


def window_kernel(bounds_ref, a_ref, b_ref, c_ref, inner_ref, outer_ref, own_ref, buf, sem):
    load_old((a_ref, b_ref, c_ref), buf, sem)
    dp = lax.axis_index("dp")
    core = lax.bitwise_and(dp, 1)
    ahead = dp * P_SIZE - bounds_ref[0]
    to_right, to_left = ahead + P_SIZE, jnp.maximum(ahead, 0) - HALF
    for i in range(3):
        inner_ref[i] = shifted(buf.at[i], jnp.where(core == 0, to_right, to_left), HROWS)
        outer_ref[i] = shifted(buf.at[i], jnp.where(core == 0, to_left, to_right), HROWS)
        own_ref[i] = shifted(buf.at[i], ahead, ROWS)


OLD_SCRATCH = (
    pltpu.VMEM((3, FRONT + CROWS + 8, LANES), jnp.float32),
    pltpu.SemaphoreType.DMA((3,)),
)


def windows(bounds, old):
    halo = jax.ShapeDtypeStruct((3, HROWS, LANES), jnp.float32)
    own = jax.ShapeDtypeStruct((3, ROWS, LANES), jnp.float32)
    return pl.pallas_call(
        window_kernel,
        in_specs=[SMEM_SPEC, ANY_SPEC, ANY_SPEC, ANY_SPEC],
        out_specs=(VMEM_SPEC,) * 3,
        out_shape=(halo, halo, own),
        scratch_shapes=list(OLD_SCRATCH),
        compiler_params=SMALL,
        cost_estimate=pl.CostEstimate(flops=10**6, bytes_accessed=16 * 10**6, transcendentals=0),
    )(bounds, *old)


def adam_kernel(
    bounds_ref, parts_ref, own_ref, inner_ref, outer_ref,
    master_ref, first_ref, second_ref, shard, grad, state,
):
    row = lax.broadcasted_iota(jnp.int32, (ROWS, LANES), 0)
    lane = lax.broadcasted_iota(jnp.int32, (ROWS, LANES), 1)
    pos = lax.axis_index("dp") * P_SIZE + row * LANES + lane
    tail = ROWS - HROWS
    first_core = lax.bitwise_and(lax.axis_index("dp"), 1) == 0
    below, above = pos[:HROWS] < bounds_ref[0], pos[tail:] >= bounds_ref[1]
    for i in range(3):
        left = jnp.where(first_core, outer_ref[i], inner_ref[i])
        right = jnp.where(first_core, inner_ref[i], outer_ref[i])
        state[i, :HROWS, :] = jnp.where(below, left, own_ref[i, :HROWS, :])
        state[i, HROWS:tail, :] = own_ref[i, HROWS:tail, :]
        state[i, tail:, :] = jnp.where(above, right, own_ref[i, tail:, :])
    for place in range(4):
        for chain in range(2):
            at = UNIT * (4 * chain + place)
            shard[:, at : at + UNIT] = parts_ref[place, chain]
    tiles = COLS // LANES
    for at in range(tiles):
        grad[pl.ds(at, 8, stride=tiles), :] = shard[:, LANES * at : LANES * (at + 1)]
    for at in range(tiles // 2):
        col = MAIN + LANES * at
        grad[pl.ds(8 * tiles + at, 8, stride=tiles // 2), :] = shard[:, col : col + LANES]
    corr_one = 1.0 - BETA_ONE**ADAM_STEP
    corr_two = 1.0 - BETA_TWO**ADAM_STEP
    g = grad[...]
    first_new = BETA_ONE * state[0] + (1.0 - BETA_ONE) * g
    second_new = BETA_TWO * state[1] + (1.0 - BETA_TWO) * g * g
    master = state[2]
    update = first_new / corr_one / (jnp.sqrt(second_new / corr_two) + EPSILON) + DECAY_RATE * master
    master_ref[...] = master - LEARN_RATE * update
    first_ref[...] = first_new
    second_ref[...] = second_new


def adam_step(bounds, parts, own, left, right):
    shape = jax.ShapeDtypeStruct((ROWS, LANES), jnp.float32)
    return pl.pallas_call(
        adam_kernel,
        in_specs=[SMEM_SPEC] + [VMEM_SPEC] * 4,
        out_specs=(VMEM_SPEC,) * 3,
        out_shape=(shape,) * 3,
        scratch_shapes=[
            pltpu.VMEM((8, SHARD_COLS), jnp.float32),
            pltpu.VMEM((ROWS, LANES), jnp.float32),
            pltpu.VMEM((3, ROWS, LANES), jnp.float32),
        ],
        compiler_params=SMALL,
        cost_estimate=pl.CostEstimate(flops=2 * 10**6, bytes_accessed=3 * 10**6, transcendentals=10**5),
    )(bounds, parts, own, left, right)


def local(tokens, cotangent, token_counts, old_bounds, old_first, old_second, old_master):
    bounds = old_bounds.reshape(2)
    old = [a.reshape(CROWS, LANES) for a in (old_first, old_second, old_master)]
    own0, own1, send0, send1 = local_gradient(tokens, cotangent, token_counts.reshape(1))
    parts, state = reduced((own0, own1), (send0, send1), bounds, old)
    outs = adam_step(bounds, parts, *state)
    return tuple(a.reshape(1, P_SIZE) for a in outs)


def solution(mesh):
    placed = (
        P(("dp", "rep"), None),
        P(("dp", "rep"), "mp"),
        P("dp", "rep"),
        P("mp", "dp", None),
        P("mp", "dp"),
        P("mp", "dp"),
        P("mp", "dp"),
    )
    return jax.shard_map(
        local,
        mesh=mesh,
        in_specs=placed,
        out_specs=(P("mp", "dp"), P("mp", "dp"), P("mp", "dp")),
        check_vma=False,
    )
```
